256 devices in a mesh: gx: 16 (over z, x_lo), gy: 16 (over x_hi, y, core).
Axes of the slice: x: 4 (x_hi: 2, x_lo: 2; x = x_hi * 2 + x_lo), y: 4, z: 8, core: 2. Of those that a mesh axis runs over, the one named last changes fastest.
Arguments:
- floe_position: float32 [16, 16, 2, 4096], P('gx', 'gy'), may hold values from 0 to 1
- floe_velocity: float32 [16, 16, 2, 4096], P('gx', 'gy'), may hold values from -4 to 4
- floe_radius: float32 [16, 16, 4096], P('gx', 'gy'), may hold values from 0.08 to 0.3
- floe_thickness: float32 [16, 16, 4096], P('gx', 'gy'), may hold values from 0.5 to 2
- tracers: float32 [16, 16, 16, 4096], P('gx', 'gy'), may hold values from 0.5 to 2
- ghost_lists: int32 [16, 16, 4, 1024], P('gx', 'gy'), may hold values from 0 to 4095
- pair_first: int32 [16, 16, 8192], P('gx', 'gy'), may hold values from 0 to 4095
- pair_second: int32 [16, 16, 8192], P('gx', 'gy'), may hold values from 0 to 8191
- pair_count: int32 [16, 16], P('gx', 'gy'), may hold values from 512 to 8192, as said below
- cell_index: int32 [16, 16, 4096], P('gx', 'gy'), may hold values from 0 to 65535
Outputs:
- new_velocity: float32 [16, 16, 2, 4096], P('gx', 'gy')
- remapped: float32 [16, 4096, 4096], P(None, 'gx', 'gy')
- smoothed: float32 [16, 4096, 4096], P(None, 'gx', 'gy')
The draws below stay inside these ranges and needn't reach their ends.
Inputs may be any that keep to these rules, and one draw needn't show every extreme that they name: Only the first pair_count slots of a block are live; some block has all 8192 slots live.
All inputs are finite; a program needn't handle non-finite values.
Results may differ from the reference program's by a relative error of at most 0.0003.
Values sent between devices are 32-bit elements; how exact they have to be, the bound alone decides.
No kernel may reach another device: no remote copies, remote signals or barrier semaphores. Data moves between devices by JAX's collectives and lax.ppermute only.
A program may use at most 64 MiB of HBM per device.

```python
import math
import jax
import jax.numpy as jnp

F_DEV = 4096
GHOST = 1024
P_DEV = 8192
CH = 16
CX = 256
CY = 256
HALO = 16
N_GX = 16
N_GY = 16


def draw_pair_count(key, part):
    levels = jax.random.randint(jax.random.fold_in(key, 11), (N_GX * N_GY,), 4, 17)
    counts = P_DEV // 256 * levels * levels
    chosen = jax.random.randint(jax.random.fold_in(key, 12), (), 0, N_GX * N_GY)
    counts = jnp.where(jnp.arange(N_GX * N_GY) == chosen, P_DEV, counts)
    return counts.reshape(N_GX, N_GY).astype(jnp.int32)


def touch_ends(values, rng, smallest, high):
    shape = values.shape
    place = [jax.random.randint(jax.random.fold_in(rng, axis), (), 0, shape[axis]) for axis in range(len(shape))]
    values = values.at[tuple(place)].set(smallest)
    longest = shape.index(max(shape))
    place[longest] = (place[longest] + 1) % shape[longest]
    return values.at[tuple(place)].set(high)


def level_of(key, extent, pieces, low, largest):
    factor_of, own = 1.0, jax.random.fold_in(key, 6)
    for dim, shards_of in pieces:
        draws = jnp.exp(jax.random.uniform(jax.random.fold_in(own, dim), (shards_of,), jnp.float32, low / len(pieces), largest / len(pieces)))
        factor_of = factor_of * jnp.repeat(draws, extent[dim] // shards_of).reshape([-1 if axis == dim else 1 for axis in range(len(extent))])
    return factor_of


def scatter_about(stream_key, shape, width, most, shards=(), held_as=jnp.bfloat16):
    array = jax.random.normal(stream_key, shape, jnp.float32) * width
    if len(shards) > 0:
        array = level_of(stream_key, shape, shards, -0.22, 0.18) * array
    return jnp.clip(array, min=-most, max=most).astype(held_as)


def setup_inputs(seed: int = 0) -> dict:
    arg_keys = jax.random.split(jax.random.key(seed), 11)
    floe_position = jnp.clip(1.0 * jax.random.uniform(arg_keys[0], (N_GX, N_GY, 2, F_DEV), jnp.float32) ** level_of(arg_keys[0], (N_GX, N_GY, 2, F_DEV), ((0, 16), (1, 16)), -0.2, 0.2), 0.0, 1.0)
    floe_velocity = scatter_about(arg_keys[1], (N_GX, N_GY, 2, F_DEV), 1.0, 4.0, ((0, 16), (1, 16)), jnp.float32)
    floe_radius = jnp.clip(jnp.exp(math.log(0.3) - 1.3217559 * jax.random.uniform(arg_keys[2], (N_GX, N_GY, F_DEV), jnp.float32) ** level_of(arg_keys[2], (N_GX, N_GY, F_DEV), ((0, 16), (1, 16)), -0.2, 0.2)), 0.08, 0.3)
    floe_thickness = jnp.clip(jnp.exp(math.log(2.0) - 1.3862944 * jax.random.uniform(arg_keys[3], (N_GX, N_GY, F_DEV), jnp.float32) ** level_of(arg_keys[3], (N_GX, N_GY, F_DEV), ((0, 16), (1, 16)), -0.2, 0.2)), 0.5, 2.0)
    tracers = jnp.clip(jnp.exp(math.log(2.0) - 1.3862944 * jax.random.uniform(arg_keys[4], (N_GX, N_GY, CH, F_DEV), jnp.float32) ** level_of(arg_keys[4], (N_GX, N_GY, CH, F_DEV), ((0, 16), (1, 16)), -0.2, 0.2)), 0.5, 2.0)
    ghost_lists = touch_ends(jax.random.randint(arg_keys[5], (N_GX, N_GY, 4, GHOST), 0, F_DEV), jax.random.fold_in(arg_keys[5], 1), 0, F_DEV - 1).astype(jnp.int32)
    pair_first = touch_ends(jax.random.randint(arg_keys[6], (N_GX, N_GY, P_DEV), 0, F_DEV), jax.random.fold_in(arg_keys[6], 1), 0, F_DEV - 1).astype(jnp.int32)
    pair_second = touch_ends(jax.random.randint(arg_keys[7], (N_GX, N_GY, P_DEV), 0, F_DEV + 4 * GHOST), jax.random.fold_in(arg_keys[7], 1), 0, (F_DEV + 4 * GHOST) - 1).astype(jnp.int32)
    pair_count = draw_pair_count(jax.random.fold_in(arg_keys[10], 71), 0)
    cell_index = touch_ends(jax.random.randint(arg_keys[9], (N_GX, N_GY, F_DEV), 0, CX * CY), jax.random.fold_in(arg_keys[9], 1), 0, (CX * CY) - 1).astype(jnp.int32)
    return dict(floe_position=floe_position, floe_velocity=floe_velocity, floe_radius=floe_radius, floe_thickness=floe_thickness, tracers=tracers, ghost_lists=ghost_lists, pair_first=pair_first, pair_second=pair_second, pair_count=pair_count, cell_index=cell_index)


stiffness = 1.0
damping = 0.2
soft_width = 0.5
core_sq = 0.0025

def contact_terms(near_floes, far_floes):
    gap_x = near_floes[0] - far_floes[0]
    gap_y = near_floes[1] - far_floes[1]
    spread = jnp.sqrt(gap_x * gap_x + gap_y * gap_y + core_sq)
    normal_x = gap_x / spread
    normal_y = gap_y / spread
    intersection = near_floes[4] + far_floes[4] - spread
    eff_radius = near_floes[4] * far_floes[4] / (near_floes[4] + far_floes[4])
    closing = (near_floes[2] - far_floes[2]) * normal_x + (near_floes[3] - far_floes[3]) * normal_y
    magnitude = eff_radius * (stiffness * soft_width * jax.nn.softplus(intersection / soft_width) - damping * closing)
    return jnp.stack([magnitude * normal_x, magnitude * normal_y, magnitude * spread])

def block_step(own_floes, ghost_table, near_index, far_index, live_count, tracer_block, cell_block):
    table = jnp.concatenate([own_floes, ghost_table], axis=1)
    near_floes = jnp.take(own_floes, near_index, axis=1)
    far_floes = jnp.take(table, far_index, axis=1)
    live = (jnp.arange(near_index.shape[0]) < live_count).astype(jnp.float32)
    terms = contact_terms(near_floes, far_floes) * live
    count = own_floes.shape[1]
    sums = jax.vmap(lambda row: jax.ops.segment_sum(row, near_index, num_segments=count))(terms)
    radius = own_floes[4]
    velocity = own_floes[2:4] + sums[0:2] / (radius * radius * own_floes[5])
    pressure = sums[2] / (radius * radius)
    values = tracer_block * pressure
    field = jax.vmap(lambda row: jax.ops.segment_sum(row, cell_block, num_segments=CX * CY))(values)
    return (velocity, field)

def reference(floe_position, floe_velocity, floe_radius, floe_thickness, tracers, ghost_lists, pair_first, pair_second, pair_count, cell_index):
    floes = jnp.concatenate([floe_position, floe_velocity, floe_radius[:, :, None], floe_thickness[:, :, None]], axis=2)

    def pick(own_floes, send_rows):
        return jnp.stack([jnp.take(own_floes, send_rows[k], axis=1) for k in range(4)])
    outgoing = jax.vmap(jax.vmap(pick))(floes, ghost_lists)
    from_left = jnp.roll(outgoing[:, :, 1], 1, axis=0)
    from_right = jnp.roll(outgoing[:, :, 0], -1, axis=0)
    empty = jnp.zeros_like(outgoing[:, :1, 3])
    from_below = jnp.concatenate([empty, outgoing[:, :-1, 3]], axis=1)
    from_above = jnp.concatenate([outgoing[:, 1:, 2], empty], axis=1)
    from_left = from_left.at[:, :, 0].add(-1.0)
    from_right = from_right.at[:, :, 0].add(1.0)
    from_below = from_below.at[:, :, 1].add(-1.0)
    from_above = from_above.at[:, :, 1].add(1.0)
    ghosts = jnp.concatenate([from_left, from_right, from_below, from_above], axis=3)
    velocity, fields = jax.vmap(jax.vmap(block_step))(floes, ghosts, pair_first, pair_second, pair_count, tracers, cell_index)
    fields = fields.reshape(N_GX, N_GY, CH, CX, CY)
    remapped = jnp.transpose(fields, (2, 0, 3, 1, 4)).reshape(CH, CX * N_GX, CY * N_GY)
    offsets = jnp.arange(2 * HALO + 1).astype(jnp.float32) - HALO
    taps = jnp.exp(-2.0 * offsets * offsets / (HALO * HALO))
    taps = taps / jnp.sum(taps)
    total_x = remapped.shape[1]
    total_y = remapped.shape[2]
    padded = jnp.concatenate([remapped[:, total_x - HALO:], remapped, remapped[:, :HALO]], axis=1)
    along_x = jnp.zeros_like(remapped)
    for step in range(2 * HALO + 1):
        along_x = along_x + taps[step] * padded[:, step:step + total_x]
    padded = jnp.pad(along_x, ((0, 0), (0, 0), (HALO, HALO)))
    smoothed = jnp.zeros_like(remapped)
    for step in range(2 * HALO + 1):
        smoothed = smoothed + taps[step] * padded[:, :, step:step + total_y]
    return (velocity, remapped, smoothed)
```

```python
import math

import jax
import jax.numpy as jnp
from jax import lax
from jax.experimental import pallas as pl
from jax.experimental.pallas import tpu as pltpu
from jax.sharding import PartitionSpec as P

F = 4096
G = 1024
NP = 8192
CH = 16
CX = 256
CY = 256
HALO = 16
MIB = 1024 * 1024

stiffness = 1.0
damping = 0.2
soft_width = 0.5
core_sq = 0.0025

TAP_TOTAL = sum(math.exp(-2.0 * (t - HALO) ** 2 / HALO**2) for t in range(2 * HALO + 1))

f32 = jnp.float32
bf16 = jnp.bfloat16
i32 = jnp.int32


def iota(shape, dim):
    return lax.broadcasted_iota(i32, shape, dim)


def row_block(start, size):
    return pl.ds(pl.multiple_of(start, size), size)


def split2(x):
    high = x.astype(bf16)
    return high, (x - high.astype(f32)).astype(bf16)


def dot_nn(a, b):
    return lax.dot_general(a, b, (((1,), (0,)), ((), ())), preferred_element_type=f32)


def dot_nt(a, b):
    return lax.dot_general(a, b, (((1,), (1,)), ((), ())), preferred_element_type=f32)


def dot3(a, b):
    ah, al = a
    bh, bl = b
    return dot_nn(ah, bh) + (dot_nn(ah, bl) + dot_nn(al, bh))


def taps_at(offset):
    o = offset.astype(f32)
    w = jnp.exp(o * o * (-2.0 / (HALO * HALO))) * (1.0 / TAP_TOTAL)
    return jnp.where(jnp.abs(offset) <= HALO, w, 0.0)


def lookup(row_of, rows, count, index, start=None):
    high = lax.shift_right_logical(index, 7)
    low = index & 127
    out = [jnp.zeros(index.shape, f32) for _ in range(rows)] if start is None else list(start)
    for h in range(count):
        here = high == h
        for r in range(rows):
            line = jnp.broadcast_to(row_of(r, h), index.shape)
            got = jnp.take_along_axis(line, low, axis=1, mode="promise_in_bounds")
            out[r] = jnp.where(here, got, out[r])
    return out


def floe_line(pos, vel, rad):
    def row_of(r, h):
        at = slice(128 * h, 128 * h + 128)
        if r < 2:
            return pos[0, 0, r : r + 1, at]
        if r < 4:
            return vel[0, 0, r - 2 : r - 1, at]
        return rad[0, 0:1, at]

    return row_of


def fetch(pairs, sem):
    copies = [pltpu.make_async_copy(a, b, sem.at[k]) for k, (a, b) in enumerate(pairs)]
    for copy in copies:
        copy.start()
    for copy in copies:
        copy.wait()


def outgoing_kernel(pos_h, vel_h, rad_h, lists_h, *refs):
    outs = refs[:4]
    pos, vel, rad, lists, lines, sem = refs[4:]
    fetch(((pos_h, pos), (vel_h, vel), (rad_h, rad), (lists_h, lists)), sem)
    row_of = floe_line(pos, vel, rad)
    for k in range(4):
        for s in range(8):
            lines[s : s + 1, :] = lists[0, 0, k : k + 1, 128 * s : 128 * s + 128]
        got = lookup(row_of, 5, 32, lines[...])
        for r in range(5):
            outs[k][8 * r : 8 * r + 8, :] = got[r]


def prepare_kernel(
    pos_h, vel_h, rad_h, tracers_h, first_h, second_h, cells_h,
    near, far, sorted_tracers, source, rows_out, cols_out, edges, uv,
    weighted, hot, cell_rows, pos, vel, rad, tracers, first, second, cells, sem,
):
    fetch(
        (
            (pos_h, pos), (vel_h, vel), (rad_h, rad), (tracers_h, tracers),
            (first_h, first), (second_h, second), (cells_h, cells),
        ),
        sem,
    )
    row_of = floe_line(pos, vel, rad)

    def gather_block(j, _):
        at = row_block(8 * j, 8)
        for index, dest in ((first, near), (second, far)):
            got = lookup(row_of, 5, 32, index[at, :])
            for r in range(5):
                dest[r, at, :] = got[r]
        return 0

    lax.fori_loop(0, 8, gather_block, 0)
    for h in range(32):
        at = slice(128 * h, 128 * h + 128)
        for r in range(2):
            uv[r, h : h + 1, :] = vel[0, 0, r : r + 1, at]

    cell = cells[...]
    bins = lax.shift_right_logical(cell, 12)
    hots = [jnp.where(bins == b, 1.0, 0.0).astype(f32) for b in range(16)]
    stacked = jnp.concatenate(hots, axis=0).astype(bf16)
    before = jnp.where(iota((128, 128), 0) < iota((128, 128), 1), 1.0, 0.0).astype(bf16)
    ones = jnp.ones((128, 128), bf16)
    inside = dot_nn(stacked, before)
    totals = dot_nn(stacked, ones).astype(bf16)
    lower = jnp.where(iota((512, 512), 1) < iota((512, 512), 0), 1.0, 0.0).astype(bf16)
    ahead = dot_nn(lower, totals)
    place = jnp.zeros((32, 128), f32)
    for b in range(16):
        at = slice(32 * b, 32 * b + 32)
        place = place + hots[b] * (ahead[at] + inside[at])
        edges[b : b + 1, :] = ahead[32 * b : 32 * b + 1].astype(i32)
    place = place.astype(i32)
    for q in range(32):
        at = slice(128 * q, 128 * q + 128)
        line = jnp.broadcast_to(place[q : q + 1, :], (128, 128))
        mine = lax.shift_right_logical(line[0:32], 7) == iota((32, 128), 0)
        weighted[0:32, at] = jnp.where(mine, float(q), 0.0).astype(bf16)
        weighted[32:64, at] = jnp.where(mine, iota((32, 128), 1).astype(f32), 0.0).astype(bf16)
        hot[:, at] = jnp.where((line & 127) == iota((128, 128), 0), 1.0, 0.0).astype(bf16)
    found = dot_nt(weighted[...], hot[...])
    source[...] = (found[0:32] * 128.0 + found[32:64]).astype(i32)

    cell_rows[...] = cell.astype(f32)
    for k in range(4):
        index = source[8 * k : 8 * k + 8, :]
        got = lookup(lambda r, h: cell_rows[h : h + 1, :], 1, 32, index)[0].astype(i32)
        for s in range(8):
            at = slice(1024 * k + 128 * s, 1024 * k + 128 * s + 128)
            rows_out[:, at] = lax.shift_right_logical(got[s : s + 1, :], 8)
            cols_out[:, at] = got[s : s + 1, :] & 255

    def tracer_block(q, _):
        index = jnp.broadcast_to(source[pl.ds(q, 1), :], (8, 128))
        high = lax.shift_right_logical(index, 7)
        low = index & 127
        parts = [jnp.zeros((8, 128), f32), jnp.zeros((8, 128), f32)]
        for h in range(32):
            here = high == h
            for c in range(2):
                block = tracers[0, 0, 8 * c : 8 * c + 8, 128 * h : 128 * h + 128]
                got = jnp.take_along_axis(block, low, axis=1, mode="promise_in_bounds")
                parts[c] = jnp.where(here, got, parts[c])
        for c in range(2):
            sorted_tracers[8 * c : 8 * c + 8, row_block(128 * q, 128)] = parts[c]
        return 0

    lax.fori_loop(0, 32, tracer_block, 0)


def pack_sides(cells, out, count, second):
    lane = iota((count, 128), 1)
    for g in range(2):
        head = jnp.zeros((count, 128), f32)
        tail = jnp.zeros((count, 128), f32)
        for k in range(8):
            mine = (lane >= 16 * k) & (lane < 16 * k + 16)
            left = cells[8 * g + k, :, 0:128]
            right = cells[8 * g + k, :, 128:256]
            head = jnp.where(mine, pltpu.roll(left, 16 * k, 1) if k else left, head)
            turn = (16 * k + 16) % 128
            tail = jnp.where(mine, pltpu.roll(right, turn, 1) if turn else right, tail)
        out[:, 128 * g : 128 * g + 128] = head
        out[:, second + 128 * g : second + 128 * g + 128] = tail


def scatter_step(step, b, c, values_high, values_low, rows_in, cols_in):
    at = row_block(256 * c, 256)
    local = jnp.broadcast_to(rows_in[:, at], (16, 256)) - 16 * b
    here = local == iota((16, 256), 0)
    columns = jnp.broadcast_to(cols_in[:, at], (256, 256))
    hot = jnp.where(columns == iota((256, 256), 0), 1.0, 0.0).astype(bf16)
    high, low = [], []
    for ch in range(CH):
        vh = jnp.broadcast_to(values_high[ch : ch + 1, at], (16, 256))
        vl = jnp.broadcast_to(values_low[ch : ch + 1, at], (16, 256))
        high.append(jnp.where(here, vh, 0.0).astype(bf16))
        low.append(jnp.where(here, vl, 0.0).astype(bf16))
    return dot_nt(jnp.concatenate(high, axis=0), hot) + dot_nt(jnp.concatenate(low, axis=0), hot)


def contact_kernel(
    count, edges_s,
    near, far, first, second, ghost0, ghost1, ghost2, ghost3, rad, thick, uv,
    sorted_tracers, source, rows_in, cols_in,
    new_velocity, values_high, values_low, head_rows, tail_rows, head_ends, tail_ends,
    weighted, hot, pressure_rows,
):
    ghosts = (ghost0, ghost1, ghost2, ghost3)
    shift = ((0, -1.0), (0, 1.0), (1, -1.0), (1, 1.0))
    live_count = count[0, 0]

    row = lax.axis_index("gy")
    inside = {2: row > 0, 3: row < lax.axis_size("gy") - 1}

    def ghost_line(r, h):
        k, s = h // 8, h % 8
        line = ghosts[k][8 * r + s : 8 * r + s + 1, :]
        if k in inside:
            line = jnp.where(jnp.full(line.shape, inside[k]), line, 0.0)
        return line + shift[k][1] if shift[k][0] == r else line

    def pair_block(j, _):
        at = row_block(8 * j, 8)
        index = second[at, :]
        outside = index >= F
        got = lookup(ghost_line, 5, 32, index - F)
        other = [jnp.where(outside, got[r], far[r, at, :]) for r in range(5)]
        own = [near[r, at, :] for r in range(5)]
        gap_x = own[0] - other[0]
        gap_y = own[1] - other[1]
        spread = jnp.sqrt(gap_x * gap_x + gap_y * gap_y + core_sq)
        normal_x = gap_x / spread
        normal_y = gap_y / spread
        reach = own[4] + other[4]
        depth = (reach - spread) / soft_width
        eff_radius = own[4] * other[4] / reach
        closing = (own[2] - other[2]) * normal_x + (own[3] - other[3]) * normal_y
        soft = jnp.maximum(depth, 0.0) + jnp.log1p(jnp.exp(-jnp.abs(depth)))
        magnitude = eff_radius * (stiffness * soft_width * soft - damping * closing)
        slot = 1024 * j + 128 * iota((8, 128), 0) + iota((8, 128), 1)
        magnitude = jnp.where(slot < live_count, magnitude, 0.0)
        terms = (magnitude * normal_x, magnitude * normal_y, magnitude * spread)
        halves = [split2(t) for t in terms]
        halves = [h[0].astype(f32) for h in halves] + [h[1].astype(f32) for h in halves]
        index = first[at, :]
        high = lax.shift_right_logical(index, 7)
        low = index & 127
        for s in range(8):
            lanes = row_block(1024 * j + 128 * s, 128)
            mine = jnp.broadcast_to(high[s : s + 1, :], (32, 128)) == iota((32, 128), 0)
            for t in range(6):
                spot = jnp.where(mine, jnp.broadcast_to(halves[t][s : s + 1, :], (32, 128)), 0.0)
                weighted[32 * t : 32 * t + 32, lanes] = spot.astype(bf16)
            match = jnp.broadcast_to(low[s : s + 1, :], (128, 128)) == iota((128, 128), 0)
            hot[:, lanes] = jnp.where(match, 1.0, 0.0).astype(bf16)
        return 0

    lax.fori_loop(0, 8, pair_block, 0)
    sums = dot_nt(weighted[...], hot[...])
    sums = [sums[32 * r : 32 * r + 32] + sums[96 + 32 * r : 128 + 32 * r] for r in range(3)]
    radius = rad[...]
    area = radius * radius
    for r in range(2):
        moved = uv[r] + sums[r] / (area * thick[...])
        for h in range(32):
            new_velocity[0, 0, r : r + 1, 128 * h : 128 * h + 128] = moved[h : h + 1, :]
    pressure_rows[...] = sums[2] / area

    def value_block(k, _):
        index = source[row_block(8 * k, 8), :]
        got = lookup(lambda r, h: pressure_rows[h : h + 1, :], 1, 32, index)[0]
        for s in range(8):
            at = row_block(1024 * k + 128 * s, 128)
            value = sorted_tracers[:, at] * jnp.broadcast_to(got[s : s + 1, :], (16, 128))
            top = value.astype(bf16).astype(f32)
            values_high[:, at] = top
            values_low[:, at] = (value - top).astype(bf16).astype(f32)
        return 0

    lax.fori_loop(0, 4, value_block, 0)

    for b, out, ends in ((0, head_rows, head_ends), (15, tail_rows, tail_ends)):
        begin = edges_s[b, 0]
        end = edges_s[1, 0] if b == 0 else F
        out[...] = jnp.zeros((CH, 16, CY), f32)

        def add_chunk(c, _, b=b, out=out):
            got = scatter_step(0, b, c, values_high, values_low, rows_in, cols_in)
            out[...] = out[...] + got.reshape(CH, 16, CY)
            return 0

        lax.fori_loop(
            lax.shift_right_logical(begin, 8), lax.shift_right_logical(end + 255, 8), add_chunk, 0
        )
        pack_sides(out, ends, 16, 256)


def grid_kernel(
    edges_s, values_high, values_low, rows_in, cols_in,
    field, sides,
):
    def step(i, carry):
        b, c, fresh = carry
        got = scatter_step(i, b, c, values_high, values_low, rows_in, cols_in)
        at = row_block(16 * b, 16)
        was = jnp.where(jnp.full((CH, 16, CY), fresh, i32) == 1, 0.0, field[:, at, :])
        field[:, at, :] = was + got.reshape(CH, 16, CY)
        following = jnp.where(b < 15, edges_s[jnp.minimum(b + 1, 15), 0], F + 1)
        up = (b < 15) & ((following <= 256 * c + 256) | (c == 15))
        return (
            jnp.where(up, b + 1, b),
            jnp.where(up, c, c + 1),
            jnp.where(up, 1, 0).astype(i32),
        )

    carry = (jnp.int32(0), jnp.int32(0), jnp.int32(1))
    for i in range(31):
        carry = step(i, carry)
    pack_sides(field, sides, CX, 256)


def own_filter_kernel(field, out, left_x, right_y):
    high, low = split2(taps_at(iota((CX, CX), 1) - iota((CX, CX), 0)))
    left_x[...] = jnp.concatenate([high, low, high], axis=1)
    right_y[...] = jnp.concatenate([high, low, high], axis=0)

    def two(k, _):
        for c in range(2):
            h, l = split2(field[2 * k + c])
            along = dot_nn(left_x[...], jnp.concatenate([h, h, l], axis=0))
            h, l = split2(along)
            out[2 * k + c] = dot_nn(jnp.concatenate([h, h, l], axis=1), right_y[...])
        return 0

    lax.fori_loop(0, CH // 2, two, 0)


def sides_kernel(own, side_l, side_r, out_h, work, sem):
    row = lax.axis_index("gy")
    ok_l, ok_r = row > 0, row < lax.axis_size("gy") - 1
    band = split2(taps_at(iota((CX, CX), 1) - iota((CX, CX), 0)))
    edge_up = split2(taps_at(iota((16, 16), 1) - 16 - iota((16, 16), 0)))
    edge_down = split2(taps_at(iota((16, 16), 1) + 16 - iota((16, 16), 0)))
    same = (iota((256, 256), 0) >> 4) == (iota((256, 256), 1) >> 4)
    delta = (iota((256, 256), 0) & 15) - (iota((256, 256), 1) & 15)
    parts = []
    for ref, ok, reach in ((side_l, ok_l, -16), (side_r, ok_r, 16)):
        rows = jnp.where(jnp.full((CX + 32, 256), ok), ref[...], 0.0)
        mid = dot3(band, split2(rows[16 : CX + 16]))
        top = mid[0:16] + dot3(edge_up, split2(rows[0:16]))
        low = mid[240:256] + dot3(edge_down, split2(rows[CX + 16 :]))
        along = jnp.concatenate([top, mid[16:240], low], axis=0)
        weights = split2(jnp.where(same, taps_at(delta + reach), 0.0))
        parts.append(dot3(split2(along), weights))
    lane = iota((CX, 128), 1)
    copies = []
    for ch in range(CH):
        g, k = ch // 8, ch % 8
        at = slice(128 * g, 128 * g + 128)
        left, right = parts[0][:, at], parts[1][:, at]
        turn = (128 - 16 * k) % 128
        left = pltpu.roll(left, turn, 1) if turn else left
        turn = (112 - 16 * k) % 128
        right = pltpu.roll(right, turn, 1) if turn else right
        work[ch, :, 0:128] = own[ch, :, 0:128] + jnp.where(lane < 16, left, 0.0)
        work[ch, :, 128:256] = own[ch, :, 128:256] + jnp.where(lane >= 112, right, 0.0)
        copy = pltpu.make_async_copy(work.at[ch], out_h.at[ch], sem.at[ch])
        copy.start()
        copies.append(copy)
    for copy in copies:
        copy.wait()


def ends_kernel(above, below, smoothed, out):
    g = pl.program_id(0)
    rows = jnp.where(jnp.full((CH, 16, CY), g, i32) == 0, above[...], below[...]).reshape(256, CY)
    band = split2(taps_at(iota((CY, CY), 1) - iota((CY, CY), 0)))
    across = dot3(split2(rows), band)
    same = (iota((256, 256), 0) >> 4) == (iota((256, 256), 1) >> 4)
    delta = (iota((256, 256), 1) & 15) - (iota((256, 256), 0) & 15)
    weights = split2(jnp.where(same, taps_at(delta + 32 * g - 16), 0.0))
    out[...] = smoothed[...] + dot3(weights, split2(across)).reshape(CH, 16, CY)


def vmem():
    return pl.BlockSpec(memory_space=pltpu.VMEM)


def anywhere():
    return pl.BlockSpec(memory_space=pl.ANY)


def smem():
    return pl.BlockSpec(memory_space=pltpu.SMEM)


def struct(*shape, dtype=f32):
    return jax.ShapeDtypeStruct(shape, dtype)


def params(mib):
    return pltpu.CompilerParams(vmem_limit_bytes=mib * MIB)


def cost(us, nbytes=1):
    return pl.CostEstimate(flops=int(us * 1.0e9), bytes_accessed=nbytes, transcendentals=0)


def shards(
    floe_position, floe_velocity, floe_radius, floe_thickness, tracers,
    ghost_lists, pair_first, pair_second, pair_count, cell_index,
):
    first = pair_first.reshape(64, 128)
    second = pair_second.reshape(64, 128)
    cells = cell_index.reshape(32, 128)
    radius = floe_radius.reshape(32, 128)
    thickness = floe_thickness.reshape(32, 128)
    nx, ny = lax.axis_size("gx"), lax.axis_size("gy")

    def ring(count):
        return [(i, (i + 1) % count) for i in range(count)]

    def back(count):
        return [((i + 1) % count, i) for i in range(count)]

    floe_scratch = [
        pltpu.VMEM((1, 1, 2, F), f32),
        pltpu.VMEM((1, 1, 2, F), f32),
        pltpu.VMEM((1, 1, F), f32),
    ]
    outgoing = pl.pallas_call(
        outgoing_kernel,
        in_specs=[anywhere()] * 4,
        out_shape=[struct(40, 128)] * 4,
        scratch_shapes=floe_scratch
        + [
            pltpu.VMEM((1, 1, 4, G), i32),
            pltpu.VMEM((8, 128), i32),
            pltpu.SemaphoreType.DMA((4,)),
        ],
        compiler_params=params(8),
        cost_estimate=cost(1),
        name="outgoing",
    )(floe_position, floe_velocity, floe_radius, ghost_lists)
    ghosts = [
        lax.ppermute(outgoing[1], "gx", ring(nx)),
        lax.ppermute(outgoing[0], "gx", back(nx)),
        lax.ppermute(outgoing[3], "gy", ring(ny)),
        lax.ppermute(outgoing[2], "gy", back(ny)),
    ]

    near, far, sorted_tracers, source, rows, cols, edges, uv = pl.pallas_call(
        prepare_kernel,
        in_specs=[anywhere()] * 7,
        out_shape=[
            struct(5, 64, 128),
            struct(5, 64, 128),
            struct(CH, F),
            struct(32, 128, dtype=i32),
            struct(1, F, dtype=i32),
            struct(1, F, dtype=i32),
            struct(16, 128, dtype=i32),
            struct(2, 32, 128),
        ],
        scratch_shapes=[
            pltpu.VMEM((64, F), bf16),
            pltpu.VMEM((128, F), bf16),
            pltpu.VMEM((32, 128), f32),
        ]
        + floe_scratch
        + [
            pltpu.VMEM((1, 1, CH, F), f32),
            pltpu.VMEM((64, 128), i32),
            pltpu.VMEM((64, 128), i32),
            pltpu.VMEM((32, 128), i32),
            pltpu.SemaphoreType.DMA((7,)),
        ],
        compiler_params=params(16),
        cost_estimate=cost(5),
        name="prepare",
    )(floe_position, floe_velocity, floe_radius, tracers, first, second, cells)

    new_velocity, values_high, values_low, head_rows, tail_rows, head_ends, tail_ends = pl.pallas_call(
        contact_kernel,
        in_specs=[smem(), smem()] + [vmem()] * 15,
        out_shape=[
            struct(1, 1, 2, F),
            struct(CH, F),
            struct(CH, F),
            struct(CH, 16, CY),
            struct(CH, 16, CY),
            struct(16, 512),
            struct(16, 512),
        ],
        scratch_shapes=[
            pltpu.VMEM((192, NP), bf16),
            pltpu.VMEM((128, NP), bf16),
            pltpu.VMEM((32, 128), f32),
        ],
        compiler_params=params(20),
        cost_estimate=cost(5),
        name="contact",
    )(
        pair_count, edges, near, far, first, second, *ghosts, radius, thickness, uv,
        sorted_tracers, source, rows, cols,
    )
    ends_above = lax.ppermute(tail_ends, "gx", ring(nx))
    ends_below = lax.ppermute(head_ends, "gx", back(nx))
    above = lax.ppermute(tail_rows, "gx", ring(nx))
    below = lax.ppermute(head_rows, "gx", back(nx))

    field, sides = pl.pallas_call(
        grid_kernel,
        in_specs=[smem()] + [vmem()] * 4,
        out_shape=[struct(CH, CX, CY), struct(CX, 512)],
        compiler_params=params(16),
        cost_estimate=cost(0.1),
        name="to_grid",
    )(edges, values_high, values_low, rows, cols)
    sides = jnp.concatenate([ends_above, sides, ends_below], axis=0)
    side_l = lax.ppermute(sides[:, 256:], "gy", ring(ny))
    side_r = lax.ppermute(sides[:, :256], "gy", back(ny))

    own = pl.pallas_call(
        own_filter_kernel,
        in_specs=[vmem()],
        out_specs=vmem(),
        out_shape=struct(CH, CX, CY),
        scratch_shapes=[pltpu.VMEM((CX, 3 * CX), bf16), pltpu.VMEM((3 * CY, CY), bf16)],
        compiler_params=params(12),
        cost_estimate=cost(0.1),
        name="own_filter",
    )(field)
    smoothed = pl.pallas_call(
        sides_kernel,
        in_specs=[vmem()] * 3,
        out_specs=anywhere(),
        out_shape=struct(CH, CX, CY),
        scratch_shapes=[pltpu.VMEM((CH, CX, CY), f32), pltpu.SemaphoreType.DMA((CH,))],
        compiler_params=params(14),
        cost_estimate=cost(0.1),
        name="add_sides",
    )(own, side_l, side_r)
    strip = pl.BlockSpec((CH, 16, CY), lambda g: (0, 15 * g, 0))
    smoothed = pl.pallas_call(
        ends_kernel,
        grid=(2,),
        in_specs=[pl.BlockSpec((CH, 16, CY), lambda g: (0, 0, 0))] * 2 + [strip],
        out_specs=strip,
        out_shape=struct(CH, CX, CY),
        input_output_aliases={2: 0},
        compiler_params=params(10),
        cost_estimate=cost(1),
        name="add_ends",
    )(above, below, smoothed)
    return (new_velocity, field, smoothed)


def solution(mesh):
    placed = (
        P("gx", "gy", None, None),
        P("gx", "gy", None, None),
        P("gx", "gy", None),
        P("gx", "gy", None),
        P("gx", "gy", None, None),
        P("gx", "gy", None, None),
        P("gx", "gy", None),
        P("gx", "gy", None),
        P("gx", "gy"),
        P("gx", "gy", None),
    )
    return jax.shard_map(
        shards,
        mesh=mesh,
        in_specs=placed,
        out_specs=(P("gx", "gy", None, None), P(None, "gx", "gy"), P(None, "gx", "gy")),
        check_vma=False,
    )
```

```python
import math

import jax
import jax.numpy as jnp
from jax import lax
from jax.experimental import pallas as pl
from jax.experimental.pallas import tpu as pltpu
from jax.sharding import PartitionSpec as P

F = 4096
G = 1024
NP = 8192
CH = 16
CX = 256
CY = 256
HALO = 16
MIB = 1024 * 1024

stiffness = 1.0
damping = 0.2
soft_width = 0.5
core_sq = 0.0025

TAP_TOTAL = sum(math.exp(-2.0 * (t - HALO) ** 2 / HALO**2) for t in range(2 * HALO + 1))

f32 = jnp.float32
bf16 = jnp.bfloat16
i32 = jnp.int32


def iota(shape, dim):
    return lax.broadcasted_iota(i32, shape, dim)


def row_block(start, size):
    return pl.ds(pl.multiple_of(start, size), size)


def split2(x):
    high = x.astype(bf16)
    return high, (x - high.astype(f32)).astype(bf16)


def dot_nn(a, b):
    return lax.dot_general(a, b, (((1,), (0,)), ((), ())), preferred_element_type=f32)


def dot_nt(a, b):
    return lax.dot_general(a, b, (((1,), (1,)), ((), ())), preferred_element_type=f32)


def left3(x):
    high, low = split2(x)
    return jnp.concatenate([high, low, high], axis=1)


def right3(x):
    high, low = split2(x)
    return jnp.concatenate([high, high, low], axis=0)


def dot3(a, b):
    return dot_nn(left3(a), right3(b))


def taps_at(offset):
    o = offset.astype(f32)
    w = jnp.exp(o * o * (-2.0 / (HALO * HALO))) * (1.0 / TAP_TOTAL)
    return jnp.where(jnp.abs(offset) <= HALO, w, 0.0)


def lookup(row_of, rows, count, index, start=None):
    high = lax.shift_right_logical(index, 7)
    low = index & 127
    out = [jnp.zeros(index.shape, f32) for _ in range(rows)] if start is None else list(start)
    for h in range(count):
        here = high == h
        for r in range(rows):
            line = jnp.broadcast_to(row_of(r, h), index.shape)
            got = jnp.take_along_axis(line, low, axis=1, mode="promise_in_bounds")
            out[r] = jnp.where(here, got, out[r])
    return out


def floe_line(pos, vel, rad):
    def row_of(r, h):
        at = slice(128 * h, 128 * h + 128)
        if r < 2:
            return pos[0, 0, r : r + 1, at]
        if r < 4:
            return vel[0, 0, r - 2 : r - 1, at]
        return rad[0, 0:1, at]

    return row_of


def fetch(pairs, sem):
    copies = [pltpu.make_async_copy(a, b, sem.at[k]) for k, (a, b) in enumerate(pairs)]
    for copy in copies:
        copy.start()
    for copy in copies:
        copy.wait()


def outgoing_kernel(pos_h, vel_h, rad_h, lists_h, *refs):
    outs = refs[:4]
    pos, vel, rad, lists, lines, sem = refs[4:]
    fetch(((pos_h, pos), (vel_h, vel), (rad_h, rad), (lists_h, lists)), sem)
    row_of = floe_line(pos, vel, rad)
    for k in range(4):
        for s in range(8):
            lines[s : s + 1, :] = lists[0, 0, k : k + 1, 128 * s : 128 * s + 128]
        got = lookup(row_of, 5, 32, lines[...])
        for r in range(5):
            outs[k][8 * r : 8 * r + 8, :] = got[r]


NEAR, FAR, SOURCE, UV, TRACERS, ROWS, COLS, PACKED = 0, 320, 640, 672, 736, 1248, 1280, 1312


def prepare_kernel(
    pos_h, vel_h, rad_h, tracers_h, first_h, second_h, cells_h,
    packed, edges,
    weighted, hot, cell_rows, source, pos, vel, rad, tracers, first, second, cells, sem,
):
    fetch(
        (
            (pos_h, pos), (vel_h, vel), (rad_h, rad), (tracers_h, tracers),
            (first_h, first), (second_h, second), (cells_h, cells),
        ),
        sem,
    )
    row_of = floe_line(pos, vel, rad)

    def gather_block(j, _):
        for index, dest in ((first, NEAR), (second, FAR)):
            got = lookup(row_of, 5, 32, index[row_block(8 * j, 8), :])
            for r in range(5):
                packed[row_block(dest + 64 * r + 8 * j, 8), :] = got[r]
        return 0

    lax.fori_loop(0, 8, gather_block, 0, unroll=8)
    for h in range(32):
        at = slice(128 * h, 128 * h + 128)
        for r in range(2):
            packed[UV + 32 * r + h : UV + 32 * r + h + 1, :] = vel[0, 0, r : r + 1, at]

    cell = cells[...]
    bins = lax.shift_right_logical(cell, 12)
    hots = [jnp.where(bins == b, 1.0, 0.0).astype(f32) for b in range(16)]
    stacked = jnp.concatenate(hots, axis=0).astype(bf16)
    before = jnp.where(iota((128, 128), 0) < iota((128, 128), 1), 1.0, 0.0).astype(bf16)
    ones = jnp.ones((128, 128), bf16)
    inside = dot_nn(stacked, before)
    totals = dot_nn(stacked, ones).astype(bf16)
    lower = jnp.where(iota((512, 512), 1) < iota((512, 512), 0), 1.0, 0.0).astype(bf16)
    ahead = dot_nn(lower, totals)
    place = jnp.zeros((32, 128), f32)
    for b in range(16):
        at = slice(32 * b, 32 * b + 32)
        place = place + hots[b] * (ahead[at] + inside[at])
        edges[b : b + 1, :] = ahead[32 * b : 32 * b + 1].astype(i32)
    place = place.astype(i32)
    for q in range(32):
        at = slice(128 * q, 128 * q + 128)
        line = jnp.broadcast_to(place[q : q + 1, :], (128, 128))
        mine = lax.shift_right_logical(line[0:32], 7) == iota((32, 128), 0)
        weighted[0:32, at] = jnp.where(mine, float(q), 0.0).astype(bf16)
        weighted[32:64, at] = jnp.where(mine, iota((32, 128), 1).astype(f32), 0.0).astype(bf16)
        hot[:, at] = jnp.where((line & 127) == iota((128, 128), 0), 1.0, 0.0).astype(bf16)
    found = dot_nt(weighted[...], hot[...])
    found = found[0:32] * 128.0 + found[32:64]
    source[...] = found.astype(i32)
    packed[SOURCE : SOURCE + 32, :] = found

    cell_rows[...] = cell.astype(f32)
    for k in range(4):
        index = source[8 * k : 8 * k + 8, :]
        got = lookup(lambda r, h: cell_rows[h : h + 1, :], 1, 32, index)[0].astype(i32)
        packed[ROWS + 8 * k : ROWS + 8 * k + 8, :] = lax.shift_right_logical(got, 8).astype(f32)
        packed[COLS + 8 * k : COLS + 8 * k + 8, :] = (got & 255).astype(f32)

    def tracer_block(q, _):
        index = jnp.broadcast_to(source[pl.ds(q, 1), :], (8, 128))
        high = lax.shift_right_logical(index, 7)
        low = index & 127
        parts = [jnp.zeros((8, 128), f32), jnp.zeros((8, 128), f32)]
        for h in range(32):
            here = high == h
            for c in range(2):
                block = tracers[0, 0, 8 * c : 8 * c + 8, 128 * h : 128 * h + 128]
                got = jnp.take_along_axis(block, low, axis=1, mode="promise_in_bounds")
                parts[c] = jnp.where(here, got, parts[c])
        for c in range(2):
            packed[row_block(TRACERS + 16 * q + 8 * c, 8), :] = parts[c]
        return 0

    lax.fori_loop(0, 32, tracer_block, 0, unroll=8)


def pack_sides(cells, out, count, second):
    lane = iota((count, 128), 1)
    for g in range(2):
        head = jnp.zeros((count, 128), f32)
        tail = jnp.zeros((count, 128), f32)
        for k in range(8):
            mine = (lane >= 16 * k) & (lane < 16 * k + 16)
            left = cells[8 * g + k, :, 0:128]
            right = cells[8 * g + k, :, 128:256]
            head = jnp.where(mine, pltpu.roll(left, 16 * k, 1) if k else left, head)
            turn = (16 * k + 16) % 128
            tail = jnp.where(mine, pltpu.roll(right, turn, 1) if turn else right, tail)
        out[:, 128 * g : 128 * g + 128] = head
        out[:, second + 128 * g : second + 128 * g + 128] = tail


def lines_at(ref, base, c):
    return jnp.concatenate([ref[pl.ds(base + 2 * c, 1), :], ref[pl.ds(base + 2 * c + 1, 1), :]], axis=1)


def scatter_step(b, c, values_high, values_low, packed):
    at = row_block(256 * c, 256)
    local = jnp.broadcast_to(lines_at(packed, ROWS, c).astype(i32) - 16 * b, (16, 256))
    here = local == iota((16, 256), 0)
    columns = jnp.broadcast_to(lines_at(packed, COLS, c).astype(i32), (256, 256))
    hot = jnp.where(columns == iota((256, 256), 0), 1.0, 0.0).astype(bf16)
    high, low = [], []
    for ch in range(CH):
        vh = jnp.broadcast_to(values_high[ch : ch + 1, at], (16, 256))
        vl = jnp.broadcast_to(values_low[ch : ch + 1, at], (16, 256))
        high.append(jnp.where(here, vh, 0.0).astype(bf16))
        low.append(jnp.where(here, vl, 0.0).astype(bf16))
    return dot_nt(jnp.concatenate(high, axis=0), hot) + dot_nt(jnp.concatenate(low, axis=0), hot)


def contact_kernel(
    count, edges_s,
    packed, first, second, ghost0, ghost1, ghost2, ghost3, rad, thick,
    new_velocity, values_high, values_low, head_rows, tail_rows,
    pressure_rows,
):
    ghosts = (ghost0, ghost1, ghost2, ghost3)
    shift = ((0, -1.0), (0, 1.0), (1, -1.0), (1, 1.0))
    live_count = count[0, 0]

    row = lax.axis_index("gy")
    inside = {2: row > 0, 3: row < lax.axis_size("gy") - 1}

    def ghost_line(r, h):
        k, s = h // 8, h % 8
        line = ghosts[k][8 * r + s : 8 * r + s + 1, :]
        if k in inside:
            line = jnp.where(jnp.full(line.shape, inside[k]), line, 0.0)
        return line + shift[k][1] if shift[k][0] == r else line

    def pair_block(j, total):
        at = row_block(8 * j, 8)
        index = second[at, :]
        outside = index >= F
        got = lookup(ghost_line, 5, 32, index - F)
        far = [packed[row_block(FAR + 64 * r + 8 * j, 8), :] for r in range(5)]
        other = [jnp.where(outside, got[r], far[r]) for r in range(5)]
        own = [packed[row_block(NEAR + 64 * r + 8 * j, 8), :] for r in range(5)]
        gap_x = own[0] - other[0]
        gap_y = own[1] - other[1]
        spread = jnp.sqrt(gap_x * gap_x + gap_y * gap_y + core_sq)
        normal_x = gap_x / spread
        normal_y = gap_y / spread
        reach = own[4] + other[4]
        depth = (reach - spread) / soft_width
        eff_radius = own[4] * other[4] / reach
        closing = (own[2] - other[2]) * normal_x + (own[3] - other[3]) * normal_y
        soft = jnp.maximum(depth, 0.0) + jnp.log1p(jnp.exp(-jnp.abs(depth)))
        magnitude = eff_radius * (stiffness * soft_width * soft - damping * closing)
        slot = 1024 * j + 128 * iota((8, 128), 0) + iota((8, 128), 1)
        magnitude = jnp.where(slot < live_count, magnitude, 0.0)
        terms = (magnitude * normal_x, magnitude * normal_y, magnitude * spread)
        halves = [split2(t) for t in terms]
        halves = [h[0].astype(f32) for h in halves] + [h[1].astype(f32) for h in halves]
        index = first[at, :]
        high = lax.shift_right_logical(index, 7)
        low = index & 127
        spots, matches = [], []
        for s in range(8):
            mine = jnp.broadcast_to(high[s : s + 1, :], (32, 128)) == iota((32, 128), 0)
            spot = [
                jnp.where(mine, jnp.broadcast_to(h[s : s + 1, :], (32, 128)), 0.0).astype(bf16)
                for h in halves
            ]
            spots.append(jnp.concatenate(spot, axis=0))
            match = jnp.broadcast_to(low[s : s + 1, :], (128, 128)) == iota((128, 128), 0)
            matches.append(jnp.where(match, 1.0, 0.0).astype(bf16))
        return total + dot_nt(jnp.concatenate(spots, axis=1), jnp.concatenate(matches, axis=1))

    sums = lax.fori_loop(0, 8, pair_block, jnp.zeros((192, 128), f32), unroll=8)
    sums = [sums[32 * r : 32 * r + 32] + sums[96 + 32 * r : 128 + 32 * r] for r in range(3)]
    radius = rad[...]
    area = radius * radius
    for r in range(2):
        moved = packed[UV + 32 * r : UV + 32 * r + 32, :] + sums[r] / (area * thick[...])
        for h in range(32):
            new_velocity[0, 0, r : r + 1, 128 * h : 128 * h + 128] = moved[h : h + 1, :]
    pressure_rows[...] = sums[2] / area

    def value_block(k, _):
        index = packed[row_block(SOURCE + 8 * k, 8), :].astype(i32)
        got = lookup(lambda r, h: pressure_rows[h : h + 1, :], 1, 32, index)[0]
        for s in range(8):
            at = row_block(1024 * k + 128 * s, 128)
            tracer = packed[row_block(TRACERS + 128 * k + 16 * s, 16), :]
            value = tracer * jnp.broadcast_to(got[s : s + 1, :], (16, 128))
            top = value.astype(bf16).astype(f32)
            values_high[:, at] = top
            values_low[:, at] = (value - top).astype(bf16).astype(f32)
        return 0

    lax.fori_loop(0, 4, value_block, 0, unroll=4)

    def both_ends(i):
        ends = ((head_rows, 0, i), (tail_rows, 15, 15 - i))
        return [(out, scatter_step(b, c, values_high, values_low, packed).reshape(CH, 16, CY)) for out, b, c in ends]

    for (out, one), (_, two) in zip(both_ends(0), both_ends(1), strict=True):
        out[...] = one + two

    def add_chunk(i, _):
        for out, got in both_ends(i):
            out[...] = out[...] + got
        return 0

    chunks = jnp.maximum(
        lax.shift_right_logical(edges_s[1, 0] + 255, 8), 16 - lax.shift_right_logical(edges_s[15, 0], 8)
    )
    lax.fori_loop(2, chunks, add_chunk, 0)


def grid_kernel(
    edges_s, values_high, values_low, packed,
    field_h, along, sides,
    field, left_x, sem,
):
    def step(i, carry):
        b, c, fresh = carry
        got = scatter_step(b, c, values_high, values_low, packed)
        at = row_block(16 * b, 16)
        was = jnp.where(jnp.full((CH, 16, CY), fresh, i32) == 1, 0.0, field[:, at, :])
        field[:, at, :] = was + got.reshape(CH, 16, CY)
        following = jnp.where(b < 15, edges_s[jnp.minimum(b + 1, 15), 0], F + 1)
        up = (b < 15) & ((following <= 256 * c + 256) | (c == 15))
        return (
            jnp.where(up, b + 1, b),
            jnp.where(up, c, c + 1),
            jnp.where(up, 1, 0).astype(i32),
        )

    carry = (jnp.int32(0), jnp.int32(0), jnp.int32(1))
    for i in range(31):
        carry = step(i, carry)
    keep = pltpu.make_async_copy(field, field_h, sem)
    keep.start()
    left_x[...] = left3(taps_at(iota((CX, CX), 1) - iota((CX, CX), 0)))

    def some(k, _):
        for c in range(4):
            along[4 * k + c] = dot_nn(left_x[...], right3(field[4 * k + c]))
        return 0

    lax.fori_loop(0, CH // 4, some, 0)
    pack_sides(along, sides, CX, 256)
    keep.wait()


def blocks_of_16(reach):
    same = (iota((256, 256), 0) >> 4) == (iota((256, 256), 1) >> 4)
    delta = (iota((256, 256), 0) & 15) - (iota((256, 256), 1) & 15)
    return jnp.where(same, taps_at(delta + reach), 0.0)


def fix_kernel(along, above, below, sides, top, low, head_cols, tail_cols, ends):
    for ref, reach, begin, out in ((above, -16, 0, top), (below, 16, CX - 16, low)):
        more = dot3(blocks_of_16(reach).T, ref[...].reshape(256, CY)).reshape(CH, 16, CY)
        out[...] = along[:, begin : begin + 16, :] + more
        pack_sides(out, ends, 16, 256)
        head_cols[begin : begin + 16, :] = ends[:, :256]
        tail_cols[begin : begin + 16, :] = ends[:, 256:]
    head_cols[16 : CX - 16, :] = sides[16 : CX - 16, :256]
    tail_cols[16 : CX - 16, :] = sides[16 : CX - 16, 256:]


def own_y_kernel(along, top, low, out, right_y):
    right_y[...] = right3(taps_at(iota((CY, CY), 1) - iota((CY, CY), 0)))

    def some(k, _):
        for c in range(4):
            ch = 4 * k + c
            rows = jnp.concatenate([top[ch], along[ch, 16 : CX - 16, :], low[ch]], axis=0)
            out[ch] = dot_nn(left3(rows), right_y[...])
        return 0

    lax.fori_loop(0, CH // 4, some, 0)


def finish_kernel(own, side_l, side_r, out_h, work, sem):
    row = lax.axis_index("gy")
    ok_l, ok_r = row > 0, row < lax.axis_size("gy") - 1
    parts = []
    for ref, ok, reach in ((side_l, ok_l, -16), (side_r, ok_r, 16)):
        columns = jnp.where(jnp.full((CX, 256), ok), ref[...], 0.0)
        parts.append(dot3(columns, blocks_of_16(reach)))
    lane = iota((CX, 128), 1)
    copies = []
    for ch in range(CH):
        g, k = ch // 8, ch % 8
        at = slice(128 * g, 128 * g + 128)
        left, right = parts[0][:, at], parts[1][:, at]
        turn = (128 - 16 * k) % 128
        left = pltpu.roll(left, turn, 1) if turn else left
        turn = (112 - 16 * k) % 128
        right = pltpu.roll(right, turn, 1) if turn else right
        work[ch, :, 0:128] = own[ch, :, 0:128] + jnp.where(lane < 16, left, 0.0)
        work[ch, :, 128:256] = own[ch, :, 128:256] + jnp.where(lane >= 112, right, 0.0)
        copy = pltpu.make_async_copy(work.at[ch], out_h.at[ch], sem.at[ch])
        copy.start()
        copies.append(copy)
    for copy in copies:
        copy.wait()


def vmem():
    return pl.BlockSpec(memory_space=pltpu.VMEM)


def anywhere():
    return pl.BlockSpec(memory_space=pl.ANY)


def hbm():
    return pl.BlockSpec(memory_space=pltpu.HBM)


def smem():
    return pl.BlockSpec(memory_space=pltpu.SMEM)


def struct(*shape, dtype=f32):
    return jax.ShapeDtypeStruct(shape, dtype)


def params(mib):
    return pltpu.CompilerParams(vmem_limit_bytes=mib * MIB)


def cost(us, nbytes=1):
    return pl.CostEstimate(flops=int(us * 1.0e9), bytes_accessed=nbytes, transcendentals=0)


def shards(
    floe_position, floe_velocity, floe_radius, floe_thickness, tracers,
    ghost_lists, pair_first, pair_second, pair_count, cell_index,
):
    first = pair_first.reshape(64, 128)
    second = pair_second.reshape(64, 128)
    cells = cell_index.reshape(32, 128)
    radius = floe_radius.reshape(32, 128)
    thickness = floe_thickness.reshape(32, 128)
    nx, ny = lax.axis_size("gx"), lax.axis_size("gy")

    def ring(count):
        return [(i, (i + 1) % count) for i in range(count)]

    def back(count):
        return [((i + 1) % count, i) for i in range(count)]

    floe_scratch = [
        pltpu.VMEM((1, 1, 2, F), f32),
        pltpu.VMEM((1, 1, 2, F), f32),
        pltpu.VMEM((1, 1, F), f32),
    ]
    outgoing = pl.pallas_call(
        outgoing_kernel,
        in_specs=[hbm()] * 4,
        out_shape=[struct(40, 128)] * 4,
        scratch_shapes=floe_scratch
        + [
            pltpu.VMEM((1, 1, 4, G), i32),
            pltpu.VMEM((8, 128), i32),
            pltpu.SemaphoreType.DMA((4,)),
        ],
        compiler_params=params(60),
        cost_estimate=cost(1),
        name="outgoing",
    )(floe_position, floe_velocity, floe_radius, ghost_lists)
    ghosts = [
        lax.ppermute(outgoing[1], "gx", ring(nx)),
        lax.ppermute(outgoing[0], "gx", back(nx)),
        lax.ppermute(outgoing[3], "gy", ring(ny)),
        lax.ppermute(outgoing[2], "gy", back(ny)),
    ]

    packed, edges = pl.pallas_call(
        prepare_kernel,
        in_specs=[hbm()] * 7,
        out_shape=[struct(PACKED, 128), struct(16, 128, dtype=i32)],
        scratch_shapes=[
            pltpu.VMEM((64, F), bf16),
            pltpu.VMEM((128, F), bf16),
            pltpu.VMEM((32, 128), f32),
            pltpu.VMEM((32, 128), i32),
        ]
        + floe_scratch
        + [
            pltpu.VMEM((1, 1, CH, F), f32),
            pltpu.VMEM((64, 128), i32),
            pltpu.VMEM((64, 128), i32),
            pltpu.VMEM((32, 128), i32),
            pltpu.SemaphoreType.DMA((7,)),
        ],
        compiler_params=params(60),
        cost_estimate=cost(5),
        name="prepare",
    )(floe_position, floe_velocity, floe_radius, tracers, first, second, cells)

    new_velocity, values_high, values_low, head_rows, tail_rows = pl.pallas_call(
        contact_kernel,
        in_specs=[smem(), smem()] + [vmem()] * 9,
        out_shape=[
            struct(1, 1, 2, F),
            struct(CH, F),
            struct(CH, F),
            struct(CH, 16, CY),
            struct(CH, 16, CY),
        ],
        scratch_shapes=[pltpu.VMEM((32, 128), f32)],
        compiler_params=params(20),
        cost_estimate=cost(5),
        name="contact",
    )(
        pair_count, edges, packed, first, second, *ghosts, radius, thickness,
    )
    above = lax.ppermute(tail_rows, "gx", ring(nx))
    below = lax.ppermute(head_rows, "gx", back(nx))

    field, along, sides = pl.pallas_call(
        grid_kernel,
        in_specs=[smem()] + [vmem()] * 3,
        out_specs=[anywhere(), vmem(), vmem()],
        out_shape=[struct(CH, CX, CY), struct(CH, CX, CY), struct(CX, 512)],
        scratch_shapes=[
            pltpu.VMEM((CH, CX, CY), f32),
            pltpu.VMEM((CX, 3 * CX), bf16),
            pltpu.SemaphoreType.DMA,
        ],
        compiler_params=params(20),
        cost_estimate=cost(10),
        name="to_grid",
    )(edges, values_high, values_low, packed)

    top, low, head_cols, tail_cols = pl.pallas_call(
        fix_kernel,
        in_specs=[vmem()] * 4,
        out_specs=[vmem()] * 4,
        out_shape=[struct(CH, 16, CY)] * 2 + [struct(CX, 256)] * 2,
        scratch_shapes=[pltpu.VMEM((16, 512), f32)],
        compiler_params=params(12),
        cost_estimate=cost(1),
        name="fix_rows",
    )(along, above, below, sides)
    side_l = lax.ppermute(tail_cols, "gy", ring(ny))
    side_r = lax.ppermute(head_cols, "gy", back(ny))

    own = pl.pallas_call(
        own_y_kernel,
        in_specs=[vmem()] * 3,
        out_specs=vmem(),
        out_shape=struct(CH, CX, CY),
        scratch_shapes=[pltpu.VMEM((3 * CY, CY), bf16)],
        compiler_params=params(12),
        cost_estimate=cost(4),
        name="own_y",
    )(along, top, low)
    smoothed = pl.pallas_call(
        finish_kernel,
        in_specs=[vmem()] * 3,
        out_specs=anywhere(),
        out_shape=struct(CH, CX, CY),
        scratch_shapes=[pltpu.VMEM((CH, CX, CY), f32), pltpu.SemaphoreType.DMA((CH,))],
        compiler_params=params(14),
        cost_estimate=cost(1),
        name="finish",
    )(own, side_l, side_r)
    return (new_velocity, field, smoothed)


def solution(mesh):
    placed = (
        P("gx", "gy", None, None),
        P("gx", "gy", None, None),
        P("gx", "gy", None),
        P("gx", "gy", None),
        P("gx", "gy", None, None),
        P("gx", "gy", None, None),
        P("gx", "gy", None),
        P("gx", "gy", None),
        P("gx", "gy"),
        P("gx", "gy", None),
    )
    return jax.shard_map(
        shards,
        mesh=mesh,
        in_specs=placed,
        out_specs=(P("gx", "gy", None, None), P(None, "gx", "gy"), P(None, "gx", "gy")),
        check_vma=False,
    )
```

```python
import math

import jax
import jax.numpy as jnp
from jax import lax
from jax.experimental import pallas as pl
from jax.experimental.pallas import tpu as pltpu
from jax.sharding import PartitionSpec as P

F = 4096
G = 1024
NP = 8192
CH = 16
CX = 256
CY = 256
HALO = 16
MIB = 1024 * 1024

stiffness = 1.0
damping = 0.2
soft_width = 0.5
core_sq = 0.0025

TAP_TOTAL = sum(math.exp(-2.0 * (t - HALO) ** 2 / HALO**2) for t in range(2 * HALO + 1))

f32 = jnp.float32
bf16 = jnp.bfloat16
i32 = jnp.int32


def iota(shape, dim):
    return lax.broadcasted_iota(i32, shape, dim)


def row_block(start, size):
    return pl.ds(pl.multiple_of(start, size), size)


def split2(x):
    high = x.astype(bf16)
    return high, (x - high.astype(f32)).astype(bf16)


def dot_nn(a, b):
    return lax.dot_general(a, b, (((1,), (0,)), ((), ())), preferred_element_type=f32)


def dot_nt(a, b):
    return lax.dot_general(a, b, (((1,), (1,)), ((), ())), preferred_element_type=f32)


def left3(x):
    high, low = split2(x)
    return jnp.concatenate([high, low, high], axis=1)


def right3(x):
    high, low = split2(x)
    return jnp.concatenate([high, high, low], axis=0)


def dot3(a, b):
    return dot_nn(left3(a), right3(b))


def taps_at(offset):
    o = offset.astype(f32)
    w = jnp.exp(o * o * (-2.0 / (HALO * HALO))) * (1.0 / TAP_TOTAL)
    return jnp.where(jnp.abs(offset) <= HALO, w, 0.0)


def lookup(row_of, rows, count, index, start=None):
    high = lax.shift_right_logical(index, 7)
    low = index & 127
    out = [jnp.zeros(index.shape, f32) for _ in range(rows)] if start is None else list(start)
    for h in range(count):
        here = high == h
        for r in range(rows):
            line = jnp.broadcast_to(row_of(r, h), index.shape)
            got = jnp.take_along_axis(line, low, axis=1, mode="promise_in_bounds")
            out[r] = jnp.where(here, got, out[r])
    return out


def floe_line(pos, vel, rad):
    def row_of(r, h):
        at = slice(128 * h, 128 * h + 128)
        if r < 2:
            return pos[0, 0, r : r + 1, at]
        if r < 4:
            return vel[0, 0, r - 2 : r - 1, at]
        return rad[0, 0:1, at]

    return row_of


def fetch(pairs, sem):
    copies = [pltpu.make_async_copy(a, b, sem.at[k]) for k, (a, b) in enumerate(pairs)]
    for copy in copies:
        copy.start()
    for copy in copies[:-1]:
        copy.wait()
    return copies[-1]


def sorted_block(tracers, source):
    index = jnp.broadcast_to(source, (8, 128))
    high = lax.shift_right_logical(index, 7)
    low = index & 127
    parts = [jnp.zeros((8, 128), f32), jnp.zeros((8, 128), f32)]
    for h in range(32):
        here = high == h
        for c in range(2):
            block = tracers[0, 0, 8 * c : 8 * c + 8, 128 * h : 128 * h + 128]
            got = jnp.take_along_axis(block, low, axis=1, mode="promise_in_bounds")
            parts[c] = jnp.where(here, got, parts[c])
    return jnp.concatenate(parts, axis=0)


def store_values(values_high, values_low, at, tracer, pressure):
    value = tracer * jnp.broadcast_to(pressure, (CH, 128))
    top = value.astype(bf16).astype(f32)
    values_high[:, at] = top
    values_low[:, at] = (value - top).astype(bf16).astype(f32)


def outgoing_kernel(pos_h, vel_h, rad_h, lists_h, *refs):
    outs = refs[:4]
    pos, vel, rad, lists, lines, sem = refs[4:]
    fetch(((pos_h, pos), (vel_h, vel), (rad_h, rad), (lists_h, lists)), sem).wait()
    row_of = floe_line(pos, vel, rad)
    for k in range(4):
        for s in range(8):
            lines[s : s + 1, :] = lists[0, 0, k : k + 1, 128 * s : 128 * s + 128]
        got = lookup(row_of, 5, 32, lines[...])
        for r in range(5):
            outs[k][8 * r : 8 * r + 8, :] = got[r]


NEAR, FAR, SOURCE, UV, TRACERS, ROWS, COLS, EDGES, PACKED = 0, 320, 640, 672, 736, 864, 896, 928, 944
EARLY = (0, 1, 2, 3, 28, 29, 30, 31)


def prepare_kernel(
    pos_h, vel_h, rad_h, tracers_h, first_h, second_h, cells_h,
    packed, edges,
    weighted, hot, cell_rows, source, pos, vel, rad, tracers, first, second, cells, sem,
):
    late = fetch(
        (
            (pos_h, pos), (vel_h, vel), (rad_h, rad), (first_h, first),
            (second_h, second), (cells_h, cells), (tracers_h, tracers),
        ),
        sem,
    )
    row_of = floe_line(pos, vel, rad)

    def gather_block(j, _):
        for index, dest in ((first, NEAR), (second, FAR)):
            got = lookup(row_of, 5, 32, index[row_block(8 * j, 8), :])
            for r in range(5):
                packed[row_block(dest + 64 * r + 8 * j, 8), :] = got[r]
        return 0

    lax.fori_loop(0, 8, gather_block, 0, unroll=8)
    for h in range(32):
        at = slice(128 * h, 128 * h + 128)
        for r in range(2):
            packed[UV + 32 * r + h : UV + 32 * r + h + 1, :] = vel[0, 0, r : r + 1, at]

    cell = cells[...]
    bins = lax.shift_right_logical(cell, 12)
    hots = [jnp.where(bins == b, 1.0, 0.0).astype(f32) for b in range(16)]
    stacked = jnp.concatenate(hots, axis=0).astype(bf16)
    before = jnp.where(iota((128, 128), 0) < iota((128, 128), 1), 1.0, 0.0).astype(bf16)
    ones = jnp.ones((128, 128), bf16)
    inside = dot_nn(stacked, before)
    totals = dot_nn(stacked, ones).astype(bf16)
    lower = jnp.where(iota((512, 512), 1) < iota((512, 512), 0), 1.0, 0.0).astype(bf16)
    ahead = dot_nn(lower, totals)
    place = jnp.zeros((32, 128), f32)
    for b in range(16):
        at = slice(32 * b, 32 * b + 32)
        place = place + hots[b] * (ahead[at] + inside[at])
        edges[b : b + 1, :] = ahead[32 * b : 32 * b + 1].astype(i32)
        packed[EDGES + b : EDGES + b + 1, :] = ahead[32 * b : 32 * b + 1]
    place = place.astype(i32)
    for q in range(32):
        at = slice(128 * q, 128 * q + 128)
        line = jnp.broadcast_to(place[q : q + 1, :], (128, 128))
        mine = lax.shift_right_logical(line[0:32], 7) == iota((32, 128), 0)
        weighted[0:32, at] = jnp.where(mine, float(q), 0.0).astype(bf16)
        weighted[32:64, at] = jnp.where(mine, iota((32, 128), 1).astype(f32), 0.0).astype(bf16)
        hot[:, at] = jnp.where((line & 127) == iota((128, 128), 0), 1.0, 0.0).astype(bf16)
    found = dot_nt(weighted[...], hot[...])
    found = found[0:32] * 128.0 + found[32:64]
    source[...] = found.astype(i32)
    packed[SOURCE : SOURCE + 32, :] = found

    cell_rows[...] = cell.astype(f32)
    for k in range(4):
        index = source[8 * k : 8 * k + 8, :]
        got = lookup(lambda r, h: cell_rows[h : h + 1, :], 1, 32, index)[0].astype(i32)
        packed[ROWS + 8 * k : ROWS + 8 * k + 8, :] = lax.shift_right_logical(got, 8).astype(f32)
        packed[COLS + 8 * k : COLS + 8 * k + 8, :] = (got & 255).astype(f32)

    late.wait()
    for t, q in enumerate(EARLY):
        packed[TRACERS + 16 * t : TRACERS + 16 * t + 16, :] = sorted_block(tracers, source[q : q + 1, :])


def pack_sides(cells, out, count, second):
    lane = iota((count, 128), 1)
    for g in range(2):
        head = jnp.zeros((count, 128), f32)
        tail = jnp.zeros((count, 128), f32)
        for k in range(8):
            mine = (lane >= 16 * k) & (lane < 16 * k + 16)
            left = cells[8 * g + k, :, 0:128]
            right = cells[8 * g + k, :, 128:256]
            head = jnp.where(mine, pltpu.roll(left, 16 * k, 1) if k else left, head)
            turn = (16 * k + 16) % 128
            tail = jnp.where(mine, pltpu.roll(right, turn, 1) if turn else right, tail)
        out[:, 128 * g : 128 * g + 128] = head
        out[:, second + 128 * g : second + 128 * g + 128] = tail


def lines_at(ref, base, c):
    return jnp.concatenate([ref[pl.ds(base + 2 * c, 1), :], ref[pl.ds(base + 2 * c + 1, 1), :]], axis=1)


def scatter_step(b, c, values_high, values_low, packed):
    at = row_block(256 * c, 256)
    local = jnp.broadcast_to(lines_at(packed, ROWS, c).astype(i32) - 16 * b, (16, 256))
    here = local == iota((16, 256), 0)
    columns = jnp.broadcast_to(lines_at(packed, COLS, c).astype(i32), (256, 256))
    hot = jnp.where(columns == iota((256, 256), 0), 1.0, 0.0).astype(bf16)
    high, low = [], []
    for ch in range(CH):
        vh = jnp.broadcast_to(values_high[ch : ch + 1, at], (16, 256))
        vl = jnp.broadcast_to(values_low[ch : ch + 1, at], (16, 256))
        high.append(jnp.where(here, vh, 0.0).astype(bf16))
        low.append(jnp.where(here, vl, 0.0).astype(bf16))
    return dot_nt(jnp.concatenate(high, axis=0), hot) + dot_nt(jnp.concatenate(low, axis=0), hot)


def contact_kernel(
    count,
    packed, first, second, ghost0, ghost1, ghost2, ghost3, rad, thick, tracers,
    new_velocity, values_high, values_low, sorted_pressure, head_rows, tail_rows,
    pressure_rows,
):
    ghosts = (ghost0, ghost1, ghost2, ghost3)
    shift = ((0, -1.0), (0, 1.0), (1, -1.0), (1, 1.0))
    live_count = count[0, 0]
    first_end = jnp.max(packed[EDGES + 1 : EDGES + 2, :]).astype(i32)
    last_begin = jnp.max(packed[EDGES + 15 : EDGES + 16, :]).astype(i32)

    row = lax.axis_index("gy")
    inside = {2: row > 0, 3: row < lax.axis_size("gy") - 1}

    def ghost_line(r, h):
        k, s = h // 8, h % 8
        line = ghosts[k][8 * r + s : 8 * r + s + 1, :]
        if k in inside:
            line = jnp.where(jnp.full(line.shape, inside[k]), line, 0.0)
        return line + shift[k][1] if shift[k][0] == r else line

    def pair_block(j, total):
        at = row_block(8 * j, 8)
        index = second[at, :]
        outside = index >= F
        got = lookup(ghost_line, 5, 32, index - F)
        far = [packed[row_block(FAR + 64 * r + 8 * j, 8), :] for r in range(5)]
        other = [jnp.where(outside, got[r], far[r]) for r in range(5)]
        own = [packed[row_block(NEAR + 64 * r + 8 * j, 8), :] for r in range(5)]
        gap_x = own[0] - other[0]
        gap_y = own[1] - other[1]
        spread = jnp.sqrt(gap_x * gap_x + gap_y * gap_y + core_sq)
        normal_x = gap_x / spread
        normal_y = gap_y / spread
        reach = own[4] + other[4]
        depth = (reach - spread) / soft_width
        eff_radius = own[4] * other[4] / reach
        closing = (own[2] - other[2]) * normal_x + (own[3] - other[3]) * normal_y
        soft = jnp.maximum(depth, 0.0) + jnp.log1p(jnp.exp(-jnp.abs(depth)))
        magnitude = eff_radius * (stiffness * soft_width * soft - damping * closing)
        slot = 1024 * j + 128 * iota((8, 128), 0) + iota((8, 128), 1)
        magnitude = jnp.where(slot < live_count, magnitude, 0.0)
        terms = (magnitude * normal_x, magnitude * normal_y, magnitude * spread)
        halves = [split2(t) for t in terms]
        halves = [h[0].astype(f32) for h in halves] + [h[1].astype(f32) for h in halves]
        index = first[at, :]
        high = lax.shift_right_logical(index, 7)
        low = index & 127
        spots, matches = [], []
        for s in range(8):
            mine = jnp.broadcast_to(high[s : s + 1, :], (32, 128)) == iota((32, 128), 0)
            spot = [
                jnp.where(mine, jnp.broadcast_to(h[s : s + 1, :], (32, 128)), 0.0).astype(bf16)
                for h in halves
            ]
            spots.append(jnp.concatenate(spot, axis=0))
            match = jnp.broadcast_to(low[s : s + 1, :], (128, 128)) == iota((128, 128), 0)
            matches.append(jnp.where(match, 1.0, 0.0).astype(bf16))
        return total + dot_nt(jnp.concatenate(spots, axis=1), jnp.concatenate(matches, axis=1))

    sums = lax.fori_loop(0, 8, pair_block, jnp.zeros((192, 128), f32), unroll=8)
    sums = [sums[32 * r : 32 * r + 32] + sums[96 + 32 * r : 128 + 32 * r] for r in range(3)]
    radius = rad[...]
    area = radius * radius
    for r in range(2):
        moved = packed[UV + 32 * r : UV + 32 * r + 32, :] + sums[r] / (area * thick[...])
        for h in range(32):
            new_velocity[0, 0, r : r + 1, 128 * h : 128 * h + 128] = moved[h : h + 1, :]
    pressure_rows[...] = sums[2] / area

    for k in range(4):
        index = packed[SOURCE + 8 * k : SOURCE + 8 * k + 8, :].astype(i32)
        got = lookup(lambda r, h: pressure_rows[h : h + 1, :], 1, 32, index)[0]
        sorted_pressure[8 * k : 8 * k + 8, :] = got
    for t, q in enumerate(EARLY):
        tracer = packed[TRACERS + 16 * t : TRACERS + 16 * t + 16, :]
        at = slice(128 * q, 128 * q + 128)
        store_values(values_high, values_low, at, tracer, sorted_pressure[q : q + 1, :])

    def both_ends(i):
        ends = ((head_rows, 0, i), (tail_rows, 15, 15 - i))
        return [(out, scatter_step(b, c, values_high, values_low, packed).reshape(CH, 16, CY)) for out, b, c in ends]

    for (out, one), (_, two) in zip(both_ends(0), both_ends(1), strict=True):
        out[...] = one + two

    def add_chunk(i, _):
        for c in (i, 15 - i):
            for q in (2 * c, 2 * c + 1):
                tracer = sorted_block(tracers, packed[pl.ds(SOURCE + q, 1), :].astype(i32))
                at = row_block(128 * q, 128)
                store_values(values_high, values_low, at, tracer, sorted_pressure[pl.ds(q, 1), :])
        for out, got in both_ends(i):
            out[...] = out[...] + got
        return 0

    chunks = jnp.maximum(
        lax.shift_right_logical(first_end + 255, 8), 16 - lax.shift_right_logical(last_begin, 8)
    )
    lax.fori_loop(2, chunks, add_chunk, 0)


def grid_kernel(
    edges_s, early_high, early_low, packed, tracers, sorted_pressure,
    field_h, along, sides,
    field, left_x, values_high, values_low, sem,
):
    for q in range(32):
        at = slice(128 * q, 128 * q + 128)
        if q in EARLY:
            values_high[:, at] = early_high[:, at]
            values_low[:, at] = early_low[:, at]
        else:
            tracer = sorted_block(tracers, packed[SOURCE + q : SOURCE + q + 1, :].astype(i32))
            store_values(values_high, values_low, at, tracer, sorted_pressure[q : q + 1, :])

    def step(i, carry):
        b, c, fresh = carry
        got = scatter_step(b, c, values_high, values_low, packed)
        at = row_block(16 * b, 16)
        was = jnp.where(jnp.full((CH, 16, CY), fresh, i32) == 1, 0.0, field[:, at, :])
        field[:, at, :] = was + got.reshape(CH, 16, CY)
        following = jnp.where(b < 15, edges_s[jnp.minimum(b + 1, 15), 0], F + 1)
        up = (b < 15) & ((following <= 256 * c + 256) | (c == 15))
        return (
            jnp.where(up, b + 1, b),
            jnp.where(up, c, c + 1),
            jnp.where(up, 1, 0).astype(i32),
        )

    carry = (jnp.int32(0), jnp.int32(0), jnp.int32(1))
    for i in range(31):
        carry = step(i, carry)
    keep = pltpu.make_async_copy(field, field_h, sem)
    keep.start()
    left_x[...] = left3(taps_at(iota((CX, CX), 1) - iota((CX, CX), 0)))

    def some(k, _):
        for c in range(4):
            along[4 * k + c] = dot_nn(left_x[...], right3(field[4 * k + c]))
        return 0

    lax.fori_loop(0, CH // 4, some, 0)
    pack_sides(along, sides, CX, 256)
    keep.wait()


def blocks_of_16(reach):
    same = (iota((256, 256), 0) >> 4) == (iota((256, 256), 1) >> 4)
    delta = (iota((256, 256), 0) & 15) - (iota((256, 256), 1) & 15)
    return jnp.where(same, taps_at(delta + reach), 0.0)


def fix_kernel(along, above, below, sides, top, low, head_cols, tail_cols, ends):
    for ref, reach, begin, out in ((above, -16, 0, top), (below, 16, CX - 16, low)):
        more = dot3(blocks_of_16(reach).T, ref[...].reshape(256, CY)).reshape(CH, 16, CY)
        out[...] = along[:, begin : begin + 16, :] + more
        pack_sides(out, ends, 16, 256)
        head_cols[begin : begin + 16, :] = ends[:, :256]
        tail_cols[begin : begin + 16, :] = ends[:, 256:]
    head_cols[16 : CX - 16, :] = sides[16 : CX - 16, :256]
    tail_cols[16 : CX - 16, :] = sides[16 : CX - 16, 256:]


def own_y_kernel(along, top, low, out, right_y):
    right_y[...] = right3(taps_at(iota((CY, CY), 1) - iota((CY, CY), 0)))

    def some(k, _):
        for c in range(4):
            ch = 4 * k + c
            rows = jnp.concatenate([top[ch], along[ch, 16 : CX - 16, :], low[ch]], axis=0)
            out[ch] = dot_nn(left3(rows), right_y[...])
        return 0

    lax.fori_loop(0, CH // 4, some, 0)


def finish_kernel(own, side_l, side_r, out_h, work, sem):
    row = lax.axis_index("gy")
    ok_l, ok_r = row > 0, row < lax.axis_size("gy") - 1
    parts = []
    for ref, ok, reach in ((side_l, ok_l, -16), (side_r, ok_r, 16)):
        columns = jnp.where(jnp.full((CX, 256), ok), ref[...], 0.0)
        parts.append(dot3(columns, blocks_of_16(reach)))
    lane = iota((CX, 128), 1)
    copies = []
    for ch in range(CH):
        g, k = ch // 8, ch % 8
        at = slice(128 * g, 128 * g + 128)
        left, right = parts[0][:, at], parts[1][:, at]
        turn = (128 - 16 * k) % 128
        left = pltpu.roll(left, turn, 1) if turn else left
        turn = (112 - 16 * k) % 128
        right = pltpu.roll(right, turn, 1) if turn else right
        work[ch, :, 0:128] = own[ch, :, 0:128] + jnp.where(lane < 16, left, 0.0)
        work[ch, :, 128:256] = own[ch, :, 128:256] + jnp.where(lane >= 112, right, 0.0)
        copy = pltpu.make_async_copy(work.at[ch], out_h.at[ch], sem.at[ch])
        copy.start()
        copies.append(copy)
    for copy in copies:
        copy.wait()


def vmem():
    return pl.BlockSpec(memory_space=pltpu.VMEM)


def anywhere():
    return pl.BlockSpec(memory_space=pl.ANY)


def hbm():
    return pl.BlockSpec(memory_space=pltpu.HBM)


def smem():
    return pl.BlockSpec(memory_space=pltpu.SMEM)


def struct(*shape, dtype=f32):
    return jax.ShapeDtypeStruct(shape, dtype)


def params(mib):
    return pltpu.CompilerParams(vmem_limit_bytes=mib * MIB)


def cost(us, nbytes=1):
    return pl.CostEstimate(flops=int(us * 1.0e9), bytes_accessed=nbytes, transcendentals=0)


def shards(
    floe_position, floe_velocity, floe_radius, floe_thickness, tracers,
    ghost_lists, pair_first, pair_second, pair_count, cell_index,
):
    first = pair_first.reshape(64, 128)
    second = pair_second.reshape(64, 128)
    cells = cell_index.reshape(32, 128)
    radius = floe_radius.reshape(32, 128)
    thickness = floe_thickness.reshape(32, 128)
    nx, ny = lax.axis_size("gx"), lax.axis_size("gy")

    def ring(count):
        return [(i, (i + 1) % count) for i in range(count)]

    def back(count):
        return [((i + 1) % count, i) for i in range(count)]

    floe_scratch = [
        pltpu.VMEM((1, 1, 2, F), f32),
        pltpu.VMEM((1, 1, 2, F), f32),
        pltpu.VMEM((1, 1, F), f32),
    ]
    outgoing = pl.pallas_call(
        outgoing_kernel,
        in_specs=[hbm()] * 4,
        out_shape=[struct(40, 128)] * 4,
        scratch_shapes=floe_scratch
        + [
            pltpu.VMEM((1, 1, 4, G), i32),
            pltpu.VMEM((8, 128), i32),
            pltpu.SemaphoreType.DMA((4,)),
        ],
        compiler_params=params(60),
        cost_estimate=cost(1),
        name="outgoing",
    )(floe_position, floe_velocity, floe_radius, ghost_lists)
    ghosts = [
        lax.ppermute(outgoing[1], "gx", ring(nx)),
        lax.ppermute(outgoing[0], "gx", back(nx)),
        lax.ppermute(outgoing[3], "gy", ring(ny)),
        lax.ppermute(outgoing[2], "gy", back(ny)),
    ]

    packed, edges = pl.pallas_call(
        prepare_kernel,
        in_specs=[hbm()] * 7,
        out_shape=[struct(PACKED, 128), struct(16, 128, dtype=i32)],
        scratch_shapes=[
            pltpu.VMEM((64, F), bf16),
            pltpu.VMEM((128, F), bf16),
            pltpu.VMEM((32, 128), f32),
            pltpu.VMEM((32, 128), i32),
        ]
        + floe_scratch
        + [
            pltpu.VMEM((1, 1, CH, F), f32),
            pltpu.VMEM((64, 128), i32),
            pltpu.VMEM((64, 128), i32),
            pltpu.VMEM((32, 128), i32),
            pltpu.SemaphoreType.DMA((7,)),
        ],
        compiler_params=params(60),
        cost_estimate=cost(5),
        name="prepare",
    )(floe_position, floe_velocity, floe_radius, tracers, first, second, cells)

    new_velocity, values_high, values_low, sorted_pressure, head_rows, tail_rows = pl.pallas_call(
        contact_kernel,
        in_specs=[smem()] + [vmem()] * 10,
        out_shape=[
            struct(1, 1, 2, F),
            struct(CH, F),
            struct(CH, F),
            struct(32, 128),
            struct(CH, 16, CY),
            struct(CH, 16, CY),
        ],
        scratch_shapes=[pltpu.VMEM((32, 128), f32)],
        compiler_params=params(20),
        cost_estimate=cost(5),
        name="contact",
    )(
        pair_count, packed, first, second, *ghosts, radius, thickness, tracers,
    )
    above = lax.ppermute(tail_rows, "gx", ring(nx))
    below = lax.ppermute(head_rows, "gx", back(nx))

    field, along, sides = pl.pallas_call(
        grid_kernel,
        in_specs=[smem()] + [vmem()] * 5,
        out_specs=[anywhere(), vmem(), vmem()],
        out_shape=[struct(CH, CX, CY), struct(CH, CX, CY), struct(CX, 512)],
        scratch_shapes=[
            pltpu.VMEM((CH, CX, CY), f32),
            pltpu.VMEM((CX, 3 * CX), bf16),
            pltpu.VMEM((CH, F), f32),
            pltpu.VMEM((CH, F), f32),
            pltpu.SemaphoreType.DMA,
        ],
        compiler_params=params(20),
        cost_estimate=cost(10),
        name="to_grid",
    )(edges, values_high, values_low, packed, tracers, sorted_pressure)

    top, low, head_cols, tail_cols = pl.pallas_call(
        fix_kernel,
        in_specs=[vmem()] * 4,
        out_specs=[vmem()] * 4,
        out_shape=[struct(CH, 16, CY)] * 2 + [struct(CX, 256)] * 2,
        scratch_shapes=[pltpu.VMEM((16, 512), f32)],
        compiler_params=params(12),
        cost_estimate=cost(1),
        name="fix_rows",
    )(along, above, below, sides)
    side_l = lax.ppermute(tail_cols, "gy", ring(ny))
    side_r = lax.ppermute(head_cols, "gy", back(ny))

    own = pl.pallas_call(
        own_y_kernel,
        in_specs=[vmem()] * 3,
        out_specs=vmem(),
        out_shape=struct(CH, CX, CY),
        scratch_shapes=[pltpu.VMEM((3 * CY, CY), bf16)],
        compiler_params=params(12),
        cost_estimate=cost(4),
        name="own_y",
    )(along, top, low)
    smoothed = pl.pallas_call(
        finish_kernel,
        in_specs=[vmem()] * 3,
        out_specs=anywhere(),
        out_shape=struct(CH, CX, CY),
        scratch_shapes=[pltpu.VMEM((CH, CX, CY), f32), pltpu.SemaphoreType.DMA((CH,))],
        compiler_params=params(14),
        cost_estimate=cost(1),
        name="finish",
    )(own, side_l, side_r)
    return (new_velocity, field, smoothed)


def solution(mesh):
    placed = (
        P("gx", "gy", None, None),
        P("gx", "gy", None, None),
        P("gx", "gy", None),
        P("gx", "gy", None),
        P("gx", "gy", None, None),
        P("gx", "gy", None, None),
        P("gx", "gy", None),
        P("gx", "gy", None),
        P("gx", "gy"),
        P("gx", "gy", None),
    )
    return jax.shard_map(
        shards,
        mesh=mesh,
        in_specs=placed,
        out_specs=(P("gx", "gy", None, None), P(None, "gx", "gy"), P(None, "gx", "gy")),
        check_vma=False,
    )
```

```python
import math

import jax
import jax.numpy as jnp
from jax import lax
from jax.experimental import pallas as pl
from jax.experimental.pallas import tpu as pltpu
from jax.sharding import PartitionSpec as P

F = 4096
G = 1024
NP = 8192
CH = 16
CX = 256
CY = 256
HALO = 16
MIB = 1024 * 1024

stiffness = 1.0
damping = 0.2
soft_width = 0.5
core_sq = 0.0025

TAP_TOTAL = sum(math.exp(-2.0 * (t - HALO) ** 2 / HALO**2) for t in range(2 * HALO + 1))

f32 = jnp.float32
bf16 = jnp.bfloat16
i32 = jnp.int32


def iota(shape, dim):
    return lax.broadcasted_iota(i32, shape, dim)


def row_block(start, size):
    return pl.ds(pl.multiple_of(start, size), size)


def split2(x):
    high = x.astype(bf16)
    return high, (x - high.astype(f32)).astype(bf16)


def dot_nn(a, b):
    return lax.dot_general(a, b, (((1,), (0,)), ((), ())), preferred_element_type=f32)


def dot_nt(a, b):
    return lax.dot_general(a, b, (((1,), (1,)), ((), ())), preferred_element_type=f32)


def left3(x):
    high, low = split2(x)
    return jnp.concatenate([high, low, high], axis=1)


def right3(x):
    high, low = split2(x)
    return jnp.concatenate([high, high, low], axis=0)


def dot3(a, b):
    return dot_nn(left3(a), right3(b))


def taps_at(offset):
    o = offset.astype(f32)
    w = jnp.exp(o * o * (-2.0 / (HALO * HALO))) * (1.0 / TAP_TOTAL)
    return jnp.where(jnp.abs(offset) <= HALO, w, 0.0)


def lookup(row_of, rows, count, index, start=None):
    high = lax.shift_right_logical(index, 7)
    low = index & 127
    out = [jnp.zeros(index.shape, f32) for _ in range(rows)] if start is None else list(start)
    for h in range(count):
        here = high == h
        for r in range(rows):
            line = jnp.broadcast_to(row_of(r, h), index.shape)
            got = jnp.take_along_axis(line, low, axis=1, mode="promise_in_bounds")
            out[r] = jnp.where(here, got, out[r])
    return out


def floe_line(pos, vel, rad):
    def row_of(r, h):
        at = slice(128 * h, 128 * h + 128)
        if r < 2:
            return pos[0, 0, r : r + 1, at]
        if r < 4:
            return vel[0, 0, r - 2 : r - 1, at]
        return rad[0, 0:1, at]

    return row_of


def fetch(pairs, sem):
    copies = [pltpu.make_async_copy(a, b, sem.at[k]) for k, (a, b) in enumerate(pairs)]
    for copy in copies:
        copy.start()
    for copy in copies[:-1]:
        copy.wait()
    return copies[-1]


def sorted_block(tracers, source):
    index = jnp.broadcast_to(source, (8, 128))
    high = lax.shift_right_logical(index, 7)
    low = index & 127
    parts = [jnp.zeros((8, 128), f32), jnp.zeros((8, 128), f32)]
    for h in range(32):
        here = high == h
        for c in range(2):
            block = tracers[0, 0, 8 * c : 8 * c + 8, 128 * h : 128 * h + 128]
            got = jnp.take_along_axis(block, low, axis=1, mode="promise_in_bounds")
            parts[c] = jnp.where(here, got, parts[c])
    return jnp.concatenate(parts, axis=0)


def store_values(values_high, values_low, at, tracer, pressure):
    value = tracer * jnp.broadcast_to(pressure, (CH, 128))
    top = value.astype(bf16).astype(f32)
    values_high[:, at] = top
    values_low[:, at] = (value - top).astype(bf16).astype(f32)


def outgoing_kernel(pos_h, vel_h, rad_h, lists_h, *refs):
    outs = refs[:4]
    pos, vel, rad, lists, lines, sem = refs[4:]
    fetch(((pos_h, pos), (vel_h, vel), (rad_h, rad), (lists_h, lists)), sem).wait()
    row_of = floe_line(pos, vel, rad)
    for k in range(4):
        for s in range(8):
            lines[s : s + 1, :] = lists[0, 0, k : k + 1, 128 * s : 128 * s + 128]
        got = lookup(row_of, 5, 32, lines[...])
        for r in range(5):
            outs[k][8 * r : 8 * r + 8, :] = got[r]


NEAR, FAR, SOURCE, UV, TRACERS, ROWS, COLS, EDGES, PACKED = 0, 320, 640, 672, 736, 864, 896, 928, 944
EARLY = (0, 1, 2, 3, 28, 29, 30, 31)


def prepare_kernel(
    pos_h, vel_h, rad_h, tracers_h, first_h, second_h, cells_h,
    packed, edges,
    weighted, hot, cell_rows, source, pos, vel, rad, tracers, first, second, cells, sem,
):
    late = fetch(
        (
            (pos_h, pos), (vel_h, vel), (rad_h, rad), (first_h, first),
            (second_h, second), (cells_h, cells), (tracers_h, tracers),
        ),
        sem,
    )
    row_of = floe_line(pos, vel, rad)

    def gather_block(j, _):
        for index, dest in ((first, NEAR), (second, FAR)):
            got = lookup(row_of, 5, 32, index[row_block(8 * j, 8), :])
            for r in range(5):
                packed[row_block(dest + 64 * r + 8 * j, 8), :] = got[r]
        return 0

    lax.fori_loop(0, 8, gather_block, 0, unroll=8)
    for h in range(32):
        at = slice(128 * h, 128 * h + 128)
        for r in range(2):
            packed[UV + 32 * r + h : UV + 32 * r + h + 1, :] = vel[0, 0, r : r + 1, at]

    cell = cells[...]
    bins = lax.shift_right_logical(cell, 12)
    hots = [jnp.where(bins == b, 1.0, 0.0).astype(f32) for b in range(16)]
    stacked = jnp.concatenate(hots, axis=0).astype(bf16)
    before = jnp.where(iota((128, 128), 0) < iota((128, 128), 1), 1.0, 0.0).astype(bf16)
    ones = jnp.ones((128, 128), bf16)
    inside = dot_nn(stacked, before)
    totals = dot_nn(stacked, ones).astype(bf16)
    lower = jnp.where(iota((512, 512), 1) < iota((512, 512), 0), 1.0, 0.0).astype(bf16)
    ahead = dot_nn(lower, totals)
    place = jnp.zeros((32, 128), f32)
    for b in range(16):
        at = slice(32 * b, 32 * b + 32)
        place = place + hots[b] * (ahead[at] + inside[at])
        edges[b : b + 1, :] = ahead[32 * b : 32 * b + 1].astype(i32)
        packed[EDGES + b : EDGES + b + 1, :] = ahead[32 * b : 32 * b + 1]
    place = place.astype(i32)
    for q in range(32):
        at = slice(128 * q, 128 * q + 128)
        line = jnp.broadcast_to(place[q : q + 1, :], (128, 128))
        mine = lax.shift_right_logical(line[0:32], 7) == iota((32, 128), 0)
        weighted[0:32, at] = jnp.where(mine, float(q), 0.0).astype(bf16)
        weighted[32:64, at] = jnp.where(mine, iota((32, 128), 1).astype(f32), 0.0).astype(bf16)
        hot[:, at] = jnp.where((line & 127) == iota((128, 128), 0), 1.0, 0.0).astype(bf16)
    found = dot_nt(weighted[...], hot[...])
    found = found[0:32] * 128.0 + found[32:64]
    source[...] = found.astype(i32)
    packed[SOURCE : SOURCE + 32, :] = found

    cell_rows[...] = cell.astype(f32)
    for k in range(4):
        index = source[8 * k : 8 * k + 8, :]
        got = lookup(lambda r, h: cell_rows[h : h + 1, :], 1, 32, index)[0].astype(i32)
        packed[ROWS + 8 * k : ROWS + 8 * k + 8, :] = lax.shift_right_logical(got, 8).astype(f32)
        packed[COLS + 8 * k : COLS + 8 * k + 8, :] = (got & 255).astype(f32)

    late.wait()
    for t, q in enumerate(EARLY):
        packed[TRACERS + 16 * t : TRACERS + 16 * t + 16, :] = sorted_block(tracers, source[q : q + 1, :])


def pack_sides(cells, heads, tails, begin, count):
    lane = iota((count, 128), 1)
    for g in range(2):
        head = jnp.zeros((count, 128), f32)
        tail = jnp.zeros((count, 128), f32)
        for k in range(8):
            mine = (lane >= 16 * k) & (lane < 16 * k + 16)
            left = cells[8 * g + k, :, 0:128]
            right = cells[8 * g + k, :, 128:256]
            head = jnp.where(mine, pltpu.roll(left, 16 * k, 1) if k else left, head)
            turn = (16 * k + 16) % 128
            tail = jnp.where(mine, pltpu.roll(right, turn, 1) if turn else right, tail)
        heads[begin : begin + count, 128 * g : 128 * g + 128] = head
        tails[begin : begin + count, 128 * g : 128 * g + 128] = tail


def lines_at(ref, base, c):
    return jnp.concatenate([ref[pl.ds(base + 2 * c, 1), :], ref[pl.ds(base + 2 * c + 1, 1), :]], axis=1)


def scatter_step(b, c, values_high, values_low, packed):
    at = row_block(256 * c, 256)
    local = jnp.broadcast_to(lines_at(packed, ROWS, c).astype(i32) - 16 * b, (16, 256))
    here = local == iota((16, 256), 0)
    columns = jnp.broadcast_to(lines_at(packed, COLS, c).astype(i32), (256, 256))
    hot = jnp.where(columns == iota((256, 256), 0), 1.0, 0.0).astype(bf16)
    high, low = [], []
    for ch in range(CH):
        vh = jnp.broadcast_to(values_high[ch : ch + 1, at], (16, 256))
        vl = jnp.broadcast_to(values_low[ch : ch + 1, at], (16, 256))
        high.append(jnp.where(here, vh, 0.0).astype(bf16))
        low.append(jnp.where(here, vl, 0.0).astype(bf16))
    return dot_nt(jnp.concatenate(high, axis=0), hot) + dot_nt(jnp.concatenate(low, axis=0), hot)


def contact_kernel(
    count,
    packed, first, second, ghost0, ghost1, ghost2, ghost3, rad, thick, tracers,
    new_velocity, values_high, values_low, sorted_pressure, head_rows, tail_rows,
    pressure_rows,
):
    ghosts = (ghost0, ghost1, ghost2, ghost3)
    shift = ((0, -1.0), (0, 1.0), (1, -1.0), (1, 1.0))
    live_count = count[0, 0]
    first_end = jnp.max(packed[EDGES + 1 : EDGES + 2, :]).astype(i32)
    last_begin = jnp.max(packed[EDGES + 15 : EDGES + 16, :]).astype(i32)

    row = lax.axis_index("gy")
    inside = {2: row > 0, 3: row < lax.axis_size("gy") - 1}

    def ghost_line(r, h):
        k, s = h // 8, h % 8
        line = ghosts[k][8 * r + s : 8 * r + s + 1, :]
        if k in inside:
            line = jnp.where(jnp.full(line.shape, inside[k]), line, 0.0)
        return line + shift[k][1] if shift[k][0] == r else line

    def pair_block(j, total):
        at = row_block(8 * j, 8)
        index = second[at, :]
        outside = index >= F
        got = lookup(ghost_line, 5, 32, index - F)
        far = [packed[row_block(FAR + 64 * r + 8 * j, 8), :] for r in range(5)]
        other = [jnp.where(outside, got[r], far[r]) for r in range(5)]
        own = [packed[row_block(NEAR + 64 * r + 8 * j, 8), :] for r in range(5)]
        gap_x = own[0] - other[0]
        gap_y = own[1] - other[1]
        spread = jnp.sqrt(gap_x * gap_x + gap_y * gap_y + core_sq)
        normal_x = gap_x / spread
        normal_y = gap_y / spread
        reach = own[4] + other[4]
        depth = (reach - spread) / soft_width
        eff_radius = own[4] * other[4] / reach
        closing = (own[2] - other[2]) * normal_x + (own[3] - other[3]) * normal_y
        soft = jnp.maximum(depth, 0.0) + jnp.log1p(jnp.exp(-jnp.abs(depth)))
        magnitude = eff_radius * (stiffness * soft_width * soft - damping * closing)
        slot = 1024 * j + 128 * iota((8, 128), 0) + iota((8, 128), 1)
        magnitude = jnp.where(slot < live_count, magnitude, 0.0)
        terms = (magnitude * normal_x, magnitude * normal_y, magnitude * spread)
        halves = [split2(t) for t in terms]
        halves = [h[0].astype(f32) for h in halves] + [h[1].astype(f32) for h in halves]
        index = first[at, :]
        high = lax.shift_right_logical(index, 7)
        low = index & 127
        spots, matches = [], []
        for s in range(8):
            mine = jnp.broadcast_to(high[s : s + 1, :], (32, 128)) == iota((32, 128), 0)
            spot = [
                jnp.where(mine, jnp.broadcast_to(h[s : s + 1, :], (32, 128)), 0.0).astype(bf16)
                for h in halves
            ]
            spots.append(jnp.concatenate(spot, axis=0))
            match = jnp.broadcast_to(low[s : s + 1, :], (128, 128)) == iota((128, 128), 0)
            matches.append(jnp.where(match, 1.0, 0.0).astype(bf16))
        return total + dot_nt(jnp.concatenate(spots, axis=1), jnp.concatenate(matches, axis=1))

    sums = lax.fori_loop(0, 8, pair_block, jnp.zeros((192, 128), f32), unroll=8)
    sums = [sums[32 * r : 32 * r + 32] + sums[96 + 32 * r : 128 + 32 * r] for r in range(3)]
    radius = rad[...]
    area = radius * radius
    for r in range(2):
        moved = packed[UV + 32 * r : UV + 32 * r + 32, :] + sums[r] / (area * thick[...])
        for h in range(32):
            new_velocity[0, 0, r : r + 1, 128 * h : 128 * h + 128] = moved[h : h + 1, :]
    pressure_rows[...] = sums[2] / area

    for k in range(4):
        index = packed[SOURCE + 8 * k : SOURCE + 8 * k + 8, :].astype(i32)
        got = lookup(lambda r, h: pressure_rows[h : h + 1, :], 1, 32, index)[0]
        sorted_pressure[8 * k : 8 * k + 8, :] = got
    for t, q in enumerate(EARLY):
        tracer = packed[TRACERS + 16 * t : TRACERS + 16 * t + 16, :]
        at = slice(128 * q, 128 * q + 128)
        store_values(values_high, values_low, at, tracer, sorted_pressure[q : q + 1, :])

    def both_ends(i):
        ends = ((head_rows, 0, i), (tail_rows, 15, 15 - i))
        return [(out, scatter_step(b, c, values_high, values_low, packed).reshape(CH, 16, CY)) for out, b, c in ends]

    for (out, one), (_, two) in zip(both_ends(0), both_ends(1), strict=True):
        out[...] = one + two

    def add_chunk(i, _):
        for c in (i, 15 - i):
            for q in (2 * c, 2 * c + 1):
                tracer = sorted_block(tracers, packed[pl.ds(SOURCE + q, 1), :].astype(i32))
                at = row_block(128 * q, 128)
                store_values(values_high, values_low, at, tracer, sorted_pressure[pl.ds(q, 1), :])
        for out, got in both_ends(i):
            out[...] = out[...] + got
        return 0

    chunks = jnp.maximum(
        lax.shift_right_logical(first_end + 255, 8), 16 - lax.shift_right_logical(last_begin, 8)
    )
    lax.fori_loop(2, chunks, add_chunk, 0)


def grid_kernel(
    edges_s, early_high, early_low, packed, tracers, sorted_pressure,
    field, head_cols, tail_cols,
    values_high, values_low,
):
    for q in range(32):
        at = slice(128 * q, 128 * q + 128)
        if q in EARLY:
            values_high[:, at] = early_high[:, at]
            values_low[:, at] = early_low[:, at]
        else:
            tracer = sorted_block(tracers, packed[SOURCE + q : SOURCE + q + 1, :].astype(i32))
            store_values(values_high, values_low, at, tracer, sorted_pressure[q : q + 1, :])

    def step(i, carry):
        b, c, fresh = carry
        got = scatter_step(b, c, values_high, values_low, packed)
        at = row_block(16 * b, 16)
        was = jnp.where(jnp.full((CH, 16, CY), fresh, i32) == 1, 0.0, field[:, at, :])
        field[:, at, :] = was + got.reshape(CH, 16, CY)
        following = jnp.where(b < 15, edges_s[jnp.minimum(b + 1, 15), 0], F + 1)
        up = (b < 15) & ((following <= 256 * c + 256) | (c == 15))
        return (
            jnp.where(up, b + 1, b),
            jnp.where(up, c, c + 1),
            jnp.where(up, 1, 0).astype(i32),
        )

    carry = (jnp.int32(0), jnp.int32(0), jnp.int32(1))
    for i in range(31):
        carry = step(i, carry)
    pack_sides(field, head_cols, tail_cols, 0, CX)


def blocks_of_16(reach):
    same = (iota((256, 256), 0) >> 4) == (iota((256, 256), 1) >> 4)
    delta = (iota((256, 256), 0) & 15) - (iota((256, 256), 1) & 15)
    return jnp.where(same, taps_at(delta + reach), 0.0)


def corners_kernel(above, below, heads, tails):
    pack_sides(above, heads, tails, 0, 16)
    pack_sides(below, heads, tails, 16, 16)


def own_kernel(field, above, below, after, out, field_h, left_x, right_y, more, sem):
    keep = pltpu.make_async_copy(field, field_h, sem)
    keep.start()
    band = taps_at(iota((CX, CX), 1) - iota((CX, CX), 0))
    left_x[...] = left3(band)
    right_y[...] = right3(band)
    for k, (ref, reach) in enumerate(((above, -16), (below, 16))):
        got = dot3(blocks_of_16(reach).T, ref[...].reshape(256, CY))
        more[k] = got.reshape(CH, 16, CY)

    def some(k, _):
        for c in range(4):
            ch = 4 * k + c
            along = dot_nn(left_x[...], right3(field[ch]))
            top = along[0:16] + more[0, ch]
            low = along[CX - 16 :] + more[1, ch]
            rows = jnp.concatenate([top, along[16 : CX - 16], low], axis=0)
            out[ch] = dot_nn(left3(rows), right_y[...])
        return 0

    lax.fori_loop(0, CH // 4, some, 0)
    keep.wait()


def finish_kernel(own, side_l, side_r, corner_l, corner_r, out_h, work, sem):
    row = lax.axis_index("gy")
    ok_l, ok_r = row > 0, row < lax.axis_size("gy") - 1
    band = left3(taps_at(iota((CX, CX), 1) - iota((CX, CX), 0)))
    edge_up = taps_at(iota((16, 16), 1) - 16 - iota((16, 16), 0))
    edge_down = taps_at(iota((16, 16), 1) + 16 - iota((16, 16), 0))
    parts = []
    for ref, corner, ok, reach in ((side_l, corner_l, ok_l, -16), (side_r, corner_r, ok_r, 16)):
        columns = jnp.where(jnp.full((CX, 256), ok), ref[...], 0.0)
        ends = jnp.where(jnp.full((32, 256), ok), corner[...], 0.0)
        mid = dot_nn(band, right3(columns))
        top = mid[0:16] + dot3(edge_up, ends[0:16])
        low = mid[CX - 16 :] + dot3(edge_down, ends[16:32])
        along = jnp.concatenate([top, mid[16 : CX - 16], low], axis=0)
        parts.append(dot3(along, blocks_of_16(reach)))
    lane = iota((CX, 128), 1)
    copies = []
    for ch in range(CH):
        g, k = ch // 8, ch % 8
        at = slice(128 * g, 128 * g + 128)
        left, right = parts[0][:, at], parts[1][:, at]
        turn = (128 - 16 * k) % 128
        left = pltpu.roll(left, turn, 1) if turn else left
        turn = (112 - 16 * k) % 128
        right = pltpu.roll(right, turn, 1) if turn else right
        work[ch, :, 0:128] = own[ch, :, 0:128] + jnp.where(lane < 16, left, 0.0)
        work[ch, :, 128:256] = own[ch, :, 128:256] + jnp.where(lane >= 112, right, 0.0)
        copy = pltpu.make_async_copy(work.at[ch], out_h.at[ch], sem.at[ch])
        copy.start()
        copies.append(copy)
    for copy in copies:
        copy.wait()


def vmem():
    return pl.BlockSpec(memory_space=pltpu.VMEM)


def anywhere():
    return pl.BlockSpec(memory_space=pl.ANY)


def hbm():
    return pl.BlockSpec(memory_space=pltpu.HBM)


def smem():
    return pl.BlockSpec(memory_space=pltpu.SMEM)


def struct(*shape, dtype=f32):
    return jax.ShapeDtypeStruct(shape, dtype)


def params(mib):
    return pltpu.CompilerParams(vmem_limit_bytes=mib * MIB)


def cost(us, nbytes=1):
    return pl.CostEstimate(flops=int(us * 1.0e9), bytes_accessed=nbytes, transcendentals=0)


def shards(
    floe_position, floe_velocity, floe_radius, floe_thickness, tracers,
    ghost_lists, pair_first, pair_second, pair_count, cell_index,
):
    first = pair_first.reshape(64, 128)
    second = pair_second.reshape(64, 128)
    cells = cell_index.reshape(32, 128)
    radius = floe_radius.reshape(32, 128)
    thickness = floe_thickness.reshape(32, 128)
    nx, ny = lax.axis_size("gx"), lax.axis_size("gy")

    def ring(count):
        return [(i, (i + 1) % count) for i in range(count)]

    def back(count):
        return [((i + 1) % count, i) for i in range(count)]

    floe_scratch = [
        pltpu.VMEM((1, 1, 2, F), f32),
        pltpu.VMEM((1, 1, 2, F), f32),
        pltpu.VMEM((1, 1, F), f32),
    ]
    outgoing = pl.pallas_call(
        outgoing_kernel,
        in_specs=[hbm()] * 4,
        out_shape=[struct(40, 128)] * 4,
        scratch_shapes=floe_scratch
        + [
            pltpu.VMEM((1, 1, 4, G), i32),
            pltpu.VMEM((8, 128), i32),
            pltpu.SemaphoreType.DMA((4,)),
        ],
        compiler_params=params(60),
        cost_estimate=cost(1),
        name="outgoing",
    )(floe_position, floe_velocity, floe_radius, ghost_lists)
    ghosts = [
        lax.ppermute(outgoing[1], "gx", ring(nx)),
        lax.ppermute(outgoing[0], "gx", back(nx)),
        lax.ppermute(outgoing[3], "gy", ring(ny)),
        lax.ppermute(outgoing[2], "gy", back(ny)),
    ]

    packed, edges = pl.pallas_call(
        prepare_kernel,
        in_specs=[hbm()] * 7,
        out_shape=[struct(PACKED, 128), struct(16, 128, dtype=i32)],
        scratch_shapes=[
            pltpu.VMEM((64, F), bf16),
            pltpu.VMEM((128, F), bf16),
            pltpu.VMEM((32, 128), f32),
            pltpu.VMEM((32, 128), i32),
        ]
        + floe_scratch
        + [
            pltpu.VMEM((1, 1, CH, F), f32),
            pltpu.VMEM((64, 128), i32),
            pltpu.VMEM((64, 128), i32),
            pltpu.VMEM((32, 128), i32),
            pltpu.SemaphoreType.DMA((7,)),
        ],
        compiler_params=params(60),
        cost_estimate=cost(5),
        name="prepare",
    )(floe_position, floe_velocity, floe_radius, tracers, first, second, cells)

    new_velocity, values_high, values_low, sorted_pressure, head_rows, tail_rows = pl.pallas_call(
        contact_kernel,
        in_specs=[smem()] + [vmem()] * 10,
        out_shape=[
            struct(1, 1, 2, F),
            struct(CH, F),
            struct(CH, F),
            struct(32, 128),
            struct(CH, 16, CY),
            struct(CH, 16, CY),
        ],
        scratch_shapes=[pltpu.VMEM((32, 128), f32)],
        compiler_params=params(20),
        cost_estimate=cost(5),
        name="contact",
    )(
        pair_count, packed, first, second, *ghosts, radius, thickness, tracers,
    )
    above = lax.ppermute(tail_rows, "gx", ring(nx))
    below = lax.ppermute(head_rows, "gx", back(nx))

    field, head_cols, tail_cols = pl.pallas_call(
        grid_kernel,
        in_specs=[smem()] + [vmem()] * 5,
        out_specs=[vmem()] * 3,
        out_shape=[struct(CH, CX, CY), struct(CX, 256), struct(CX, 256)],
        scratch_shapes=[pltpu.VMEM((CH, F), f32), pltpu.VMEM((CH, F), f32)],
        compiler_params=params(16),
        cost_estimate=cost(8),
        name="to_grid",
    )(edges, values_high, values_low, packed, tracers, sorted_pressure)
    side_l = lax.ppermute(tail_cols, "gy", ring(ny))
    side_r = lax.ppermute(head_cols, "gy", back(ny))

    corner_heads, corner_tails = pl.pallas_call(
        corners_kernel,
        in_specs=[vmem()] * 2,
        out_specs=[vmem()] * 2,
        out_shape=[struct(32, 256)] * 2,
        compiler_params=params(4),
        cost_estimate=cost(0.2),
        name="corners",
    )(above, below)
    corner_l = lax.ppermute(corner_tails, "gy", ring(ny))
    corner_r = lax.ppermute(corner_heads, "gy", back(ny))

    own, field = pl.pallas_call(
        own_kernel,
        in_specs=[vmem()] * 4,
        out_specs=[vmem(), hbm()],
        out_shape=[struct(CH, CX, CY)] * 2,
        scratch_shapes=[
            pltpu.VMEM((CX, 3 * CX), bf16),
            pltpu.VMEM((3 * CY, CY), bf16),
            pltpu.VMEM((2, CH, 16, CY), f32),
            pltpu.SemaphoreType.DMA,
        ],
        compiler_params=params(12),
        cost_estimate=cost(6),
        name="own_filters",
    )(field, above, below, corner_heads)
    smoothed = pl.pallas_call(
        finish_kernel,
        in_specs=[vmem()] * 5,
        out_specs=anywhere(),
        out_shape=struct(CH, CX, CY),
        scratch_shapes=[pltpu.VMEM((CH, CX, CY), f32), pltpu.SemaphoreType.DMA((CH,))],
        compiler_params=params(14),
        cost_estimate=cost(1),
        name="finish",
    )(own, side_l, side_r, corner_l, corner_r)
    return (new_velocity, field, smoothed)


def solution(mesh):
    placed = (
        P("gx", "gy", None, None),
        P("gx", "gy", None, None),
        P("gx", "gy", None),
        P("gx", "gy", None),
        P("gx", "gy", None, None),
        P("gx", "gy", None, None),
        P("gx", "gy", None),
        P("gx", "gy", None),
        P("gx", "gy"),
        P("gx", "gy", None),
    )
    return jax.shard_map(
        shards,
        mesh=mesh,
        in_specs=placed,
        out_specs=(P("gx", "gy", None, None), P(None, "gx", "gy"), P(None, "gx", "gy")),
        check_vma=False,
    )
```

```python
import math

import jax
import jax.numpy as jnp
from jax import lax
from jax.experimental import pallas as pl
from jax.experimental.pallas import tpu as pltpu
from jax.sharding import PartitionSpec as P

F = 4096
G = 1024
NP = 8192
CH = 16
CX = 256
CY = 256
HALO = 16
MIB = 1024 * 1024

stiffness = 1.0
damping = 0.2
soft_width = 0.5
core_sq = 0.0025

TAP_TOTAL = sum(math.exp(-2.0 * (t - HALO) ** 2 / HALO**2) for t in range(2 * HALO + 1))

f32 = jnp.float32
bf16 = jnp.bfloat16
i32 = jnp.int32


def iota(shape, dim):
    return lax.broadcasted_iota(i32, shape, dim)


def row_block(start, size):
    return pl.ds(pl.multiple_of(start, size), size)


def split2(x):
    high = x.astype(bf16)
    return high, (x - high.astype(f32)).astype(bf16)


def dot_nn(a, b):
    return lax.dot_general(a, b, (((1,), (0,)), ((), ())), preferred_element_type=f32)


def dot_nt(a, b):
    return lax.dot_general(a, b, (((1,), (1,)), ((), ())), preferred_element_type=f32)


def left3(x):
    high, low = split2(x)
    return jnp.concatenate([high, low, high], axis=1)


def right3(x):
    high, low = split2(x)
    return jnp.concatenate([high, high, low], axis=0)


def dot3(a, b):
    return dot_nn(left3(a), right3(b))


def taps_at(offset):
    o = offset.astype(f32)
    w = jnp.exp(o * o * (-2.0 / (HALO * HALO))) * (1.0 / TAP_TOTAL)
    return jnp.where(jnp.abs(offset) <= HALO, w, 0.0)


def lookup(row_of, rows, count, index, start=None):
    high = lax.shift_right_logical(index, 7)
    low = index & 127
    out = [jnp.zeros(index.shape, f32) for _ in range(rows)] if start is None else list(start)
    for h in range(count):
        here = high == h
        for r in range(rows):
            line = jnp.broadcast_to(row_of(r, h), index.shape)
            got = jnp.take_along_axis(line, low, axis=1, mode="promise_in_bounds")
            out[r] = jnp.where(here, got, out[r])
    return out


def floe_line(pos, vel, rad):
    def row_of(r, h):
        at = slice(128 * h, 128 * h + 128)
        if r < 2:
            return pos[0, 0, r : r + 1, at]
        if r < 4:
            return vel[0, 0, r - 2 : r - 1, at]
        return rad[0, 0:1, at]

    return row_of


def fetch(pairs, sem):
    copies = [pltpu.make_async_copy(a, b, sem.at[k]) for k, (a, b) in enumerate(pairs)]
    for copy in copies:
        copy.start()
    for copy in copies[:-1]:
        copy.wait()
    return copies[-1]


def sorted_block(tracers, source):
    index = jnp.broadcast_to(source, (8, 128))
    high = lax.shift_right_logical(index, 7)
    low = index & 127
    parts = [jnp.zeros((8, 128), f32), jnp.zeros((8, 128), f32)]
    for h in range(32):
        here = high == h
        for c in range(2):
            block = tracers[0, 0, 8 * c : 8 * c + 8, 128 * h : 128 * h + 128]
            got = jnp.take_along_axis(block, low, axis=1, mode="promise_in_bounds")
            parts[c] = jnp.where(here, got, parts[c])
    return jnp.concatenate(parts, axis=0)


def store_values(values_high, values_low, at, tracer, pressure):
    value = tracer * jnp.broadcast_to(pressure, (CH, 128))
    top = value.astype(bf16).astype(f32)
    values_high[:, at] = top
    values_low[:, at] = (value - top).astype(bf16).astype(f32)


def outgoing_kernel(pos_h, vel_h, rad_h, lists_h, *refs):
    outs = refs[:4]
    pos, vel, rad, lists, lines, sem = refs[4:]
    fetch(((pos_h, pos), (vel_h, vel), (rad_h, rad), (lists_h, lists)), sem).wait()
    row_of = floe_line(pos, vel, rad)
    for k in range(4):
        for s in range(8):
            lines[s : s + 1, :] = lists[0, 0, k : k + 1, 128 * s : 128 * s + 128]
        got = lookup(row_of, 5, 32, lines[...])
        for r in range(5):
            outs[k][8 * r : 8 * r + 8, :] = got[r]


NEAR, FAR, SOURCE, UV, TRACERS, ROWS, COLS, EDGES, PACKED = 0, 320, 640, 672, 736, 864, 896, 928, 944
EARLY = (0, 1, 2, 3, 28, 29, 30, 31)


def prepare_kernel(
    pos_h, vel_h, rad_h, tracers_h, first_h, second_h, cells_h,
    packed, edges,
    weighted, hot, cell_rows, source, pos, vel, rad, tracers, first, second, cells, sem,
):
    late = fetch(
        (
            (pos_h, pos), (vel_h, vel), (rad_h, rad), (first_h, first),
            (second_h, second), (cells_h, cells), (tracers_h, tracers),
        ),
        sem,
    )
    row_of = floe_line(pos, vel, rad)

    def gather_block(j, _):
        for index, dest in ((first, NEAR), (second, FAR)):
            got = lookup(row_of, 5, 32, index[row_block(8 * j, 8), :])
            for r in range(5):
                packed[row_block(dest + 64 * r + 8 * j, 8), :] = got[r]
        return 0

    lax.fori_loop(0, 8, gather_block, 0, unroll=8)
    for h in range(32):
        at = slice(128 * h, 128 * h + 128)
        for r in range(2):
            packed[UV + 32 * r + h : UV + 32 * r + h + 1, :] = vel[0, 0, r : r + 1, at]

    cell = cells[...]
    bins = lax.shift_right_logical(cell, 12)
    hots = [jnp.where(bins == b, 1.0, 0.0).astype(f32) for b in range(16)]
    stacked = jnp.concatenate(hots, axis=0).astype(bf16)
    before = jnp.where(iota((128, 128), 0) < iota((128, 128), 1), 1.0, 0.0).astype(bf16)
    ones = jnp.ones((128, 128), bf16)
    inside = dot_nn(stacked, before)
    totals = dot_nn(stacked, ones).astype(bf16)
    lower = jnp.where(iota((512, 512), 1) < iota((512, 512), 0), 1.0, 0.0).astype(bf16)
    ahead = dot_nn(lower, totals)
    place = jnp.zeros((32, 128), f32)
    for b in range(16):
        at = slice(32 * b, 32 * b + 32)
        place = place + hots[b] * (ahead[at] + inside[at])
        edges[b : b + 1, :] = ahead[32 * b : 32 * b + 1].astype(i32)
        packed[EDGES + b : EDGES + b + 1, :] = ahead[32 * b : 32 * b + 1]
    place = place.astype(i32)
    for q in range(32):
        at = slice(128 * q, 128 * q + 128)
        line = jnp.broadcast_to(place[q : q + 1, :], (128, 128))
        mine = lax.shift_right_logical(line[0:32], 7) == iota((32, 128), 0)
        weighted[0:32, at] = jnp.where(mine, float(q), 0.0).astype(bf16)
        weighted[32:64, at] = jnp.where(mine, iota((32, 128), 1).astype(f32), 0.0).astype(bf16)
        hot[:, at] = jnp.where((line & 127) == iota((128, 128), 0), 1.0, 0.0).astype(bf16)
    found = dot_nt(weighted[...], hot[...])
    found = found[0:32] * 128.0 + found[32:64]
    source[...] = found.astype(i32)
    packed[SOURCE : SOURCE + 32, :] = found

    cell_rows[...] = cell.astype(f32)
    for k in range(4):
        index = source[8 * k : 8 * k + 8, :]
        got = lookup(lambda r, h: cell_rows[h : h + 1, :], 1, 32, index)[0].astype(i32)
        packed[ROWS + 8 * k : ROWS + 8 * k + 8, :] = lax.shift_right_logical(got, 8).astype(f32)
        packed[COLS + 8 * k : COLS + 8 * k + 8, :] = (got & 255).astype(f32)

    late.wait()
    for t, q in enumerate(EARLY):
        packed[TRACERS + 16 * t : TRACERS + 16 * t + 16, :] = sorted_block(tracers, source[q : q + 1, :])


def pack_sides(cells, out, count, second):
    lane = iota((count, 128), 1)
    for g in range(2):
        head = jnp.zeros((count, 128), f32)
        tail = jnp.zeros((count, 128), f32)
        for k in range(8):
            mine = (lane >= 16 * k) & (lane < 16 * k + 16)
            left = cells[8 * g + k, :, 0:128]
            right = cells[8 * g + k, :, 128:256]
            head = jnp.where(mine, pltpu.roll(left, 16 * k, 1) if k else left, head)
            turn = (16 * k + 16) % 128
            tail = jnp.where(mine, pltpu.roll(right, turn, 1) if turn else right, tail)
        out[:, 128 * g : 128 * g + 128] = head
        out[:, second + 128 * g : second + 128 * g + 128] = tail


def lines_at(ref, base, c):
    return jnp.concatenate([ref[pl.ds(base + 2 * c, 1), :], ref[pl.ds(base + 2 * c + 1, 1), :]], axis=1)


def scatter_step(b, c, values_high, values_low, packed):
    at = row_block(256 * c, 256)
    local = jnp.broadcast_to(lines_at(packed, ROWS, c).astype(i32) - 16 * b, (16, 256))
    here = local == iota((16, 256), 0)
    columns = jnp.broadcast_to(lines_at(packed, COLS, c).astype(i32), (256, 256))
    hot = jnp.where(columns == iota((256, 256), 0), 1.0, 0.0).astype(bf16)
    high, low = [], []
    for ch in range(CH):
        vh = jnp.broadcast_to(values_high[ch : ch + 1, at], (16, 256))
        vl = jnp.broadcast_to(values_low[ch : ch + 1, at], (16, 256))
        high.append(jnp.where(here, vh, 0.0).astype(bf16))
        low.append(jnp.where(here, vl, 0.0).astype(bf16))
    return dot_nt(jnp.concatenate(high, axis=0), hot) + dot_nt(jnp.concatenate(low, axis=0), hot)


def contact_kernel(
    count,
    packed, first, second, ghost2, ghost3, ghost0, ghost1, rad, thick, tracers,
    new_velocity, values_high, values_low, sorted_pressure, head_rows, tail_rows,
    pressure_rows,
):
    ghosts = (ghost0, ghost1, ghost2, ghost3)
    shift = ((0, -1.0), (0, 1.0), (1, -1.0), (1, 1.0))
    live_count = count[0, 0]
    first_end = jnp.max(packed[EDGES + 1 : EDGES + 2, :]).astype(i32)
    last_begin = jnp.max(packed[EDGES + 15 : EDGES + 16, :]).astype(i32)

    row = lax.axis_index("gy")
    inside = {2: row > 0, 3: row < lax.axis_size("gy") - 1}

    def ghost_line(r, h):
        k, s = h // 8, h % 8
        line = ghosts[k][8 * r + s : 8 * r + s + 1, :]
        if k in inside:
            line = jnp.where(jnp.full(line.shape, inside[k]), line, 0.0)
        return line + shift[k][1] if shift[k][0] == r else line

    def pair_block(j, total):
        at = row_block(8 * j, 8)
        index = second[at, :]
        outside = index >= F
        got = lookup(ghost_line, 5, 32, index - F)
        far = [packed[row_block(FAR + 64 * r + 8 * j, 8), :] for r in range(5)]
        other = [jnp.where(outside, got[r], far[r]) for r in range(5)]
        own = [packed[row_block(NEAR + 64 * r + 8 * j, 8), :] for r in range(5)]
        gap_x = own[0] - other[0]
        gap_y = own[1] - other[1]
        spread = jnp.sqrt(gap_x * gap_x + gap_y * gap_y + core_sq)
        normal_x = gap_x / spread
        normal_y = gap_y / spread
        reach = own[4] + other[4]
        depth = (reach - spread) / soft_width
        eff_radius = own[4] * other[4] / reach
        closing = (own[2] - other[2]) * normal_x + (own[3] - other[3]) * normal_y
        soft = jnp.maximum(depth, 0.0) + jnp.log1p(jnp.exp(-jnp.abs(depth)))
        magnitude = eff_radius * (stiffness * soft_width * soft - damping * closing)
        slot = 1024 * j + 128 * iota((8, 128), 0) + iota((8, 128), 1)
        magnitude = jnp.where(slot < live_count, magnitude, 0.0)
        terms = (magnitude * normal_x, magnitude * normal_y, magnitude * spread)
        halves = [split2(t) for t in terms]
        halves = [h[0].astype(f32) for h in halves] + [h[1].astype(f32) for h in halves]
        index = first[at, :]
        high = lax.shift_right_logical(index, 7)
        low = index & 127
        spots, matches = [], []
        for s in range(8):
            mine = jnp.broadcast_to(high[s : s + 1, :], (32, 128)) == iota((32, 128), 0)
            spot = [
                jnp.where(mine, jnp.broadcast_to(h[s : s + 1, :], (32, 128)), 0.0).astype(bf16)
                for h in halves
            ]
            spots.append(jnp.concatenate(spot, axis=0))
            match = jnp.broadcast_to(low[s : s + 1, :], (128, 128)) == iota((128, 128), 0)
            matches.append(jnp.where(match, 1.0, 0.0).astype(bf16))
        return total + dot_nt(jnp.concatenate(spots, axis=1), jnp.concatenate(matches, axis=1))

    sums = lax.fori_loop(0, 8, pair_block, jnp.zeros((192, 128), f32), unroll=8)
    sums = [sums[32 * r : 32 * r + 32] + sums[96 + 32 * r : 128 + 32 * r] for r in range(3)]
    radius = rad[...]
    area = radius * radius
    for r in range(2):
        moved = packed[UV + 32 * r : UV + 32 * r + 32, :] + sums[r] / (area * thick[...])
        for h in range(32):
            new_velocity[0, 0, r : r + 1, 128 * h : 128 * h + 128] = moved[h : h + 1, :]
    pressure_rows[...] = sums[2] / area

    for k in range(4):
        index = packed[SOURCE + 8 * k : SOURCE + 8 * k + 8, :].astype(i32)
        got = lookup(lambda r, h: pressure_rows[h : h + 1, :], 1, 32, index)[0]
        sorted_pressure[8 * k : 8 * k + 8, :] = got
    for t, q in enumerate(EARLY):
        tracer = packed[TRACERS + 16 * t : TRACERS + 16 * t + 16, :]
        at = slice(128 * q, 128 * q + 128)
        store_values(values_high, values_low, at, tracer, sorted_pressure[q : q + 1, :])

    def both_ends(i):
        ends = ((head_rows, 0, i), (tail_rows, 15, 15 - i))
        return [(out, scatter_step(b, c, values_high, values_low, packed).reshape(CH, 16, CY)) for out, b, c in ends]

    for (out, one), (_, two) in zip(both_ends(0), both_ends(1), strict=True):
        out[...] = one + two

    def add_chunk(i, _):
        for c in (i, 15 - i):
            for q in (2 * c, 2 * c + 1):
                tracer = sorted_block(tracers, packed[pl.ds(SOURCE + q, 1), :].astype(i32))
                at = row_block(128 * q, 128)
                store_values(values_high, values_low, at, tracer, sorted_pressure[pl.ds(q, 1), :])
        for out, got in both_ends(i):
            out[...] = out[...] + got
        return 0

    chunks = jnp.maximum(
        lax.shift_right_logical(first_end + 255, 8), 16 - lax.shift_right_logical(last_begin, 8)
    )
    lax.fori_loop(2, chunks, add_chunk, 0)


def grid_kernel(
    edges_s, early_high, early_low, packed, tracers, sorted_pressure,
    field_h, along, sides,
    field, left_x, values_high, values_low, sem,
):
    for q in range(32):
        at = slice(128 * q, 128 * q + 128)
        if q in EARLY:
            values_high[:, at] = early_high[:, at]
            values_low[:, at] = early_low[:, at]
        else:
            tracer = sorted_block(tracers, packed[SOURCE + q : SOURCE + q + 1, :].astype(i32))
            store_values(values_high, values_low, at, tracer, sorted_pressure[q : q + 1, :])

    def step(i, carry):
        b, c, fresh = carry
        got = scatter_step(b, c, values_high, values_low, packed)
        at = row_block(16 * b, 16)
        was = jnp.where(jnp.full((CH, 16, CY), fresh, i32) == 1, 0.0, field[:, at, :])
        field[:, at, :] = was + got.reshape(CH, 16, CY)
        following = jnp.where(b < 15, edges_s[jnp.minimum(b + 1, 15), 0], F + 1)
        up = (b < 15) & ((following <= 256 * c + 256) | (c == 15))
        return (
            jnp.where(up, b + 1, b),
            jnp.where(up, c, c + 1),
            jnp.where(up, 1, 0).astype(i32),
        )

    carry = (jnp.int32(0), jnp.int32(0), jnp.int32(1))
    for i in range(31):
        carry = step(i, carry)
    keep = pltpu.make_async_copy(field, field_h, sem)
    keep.start()
    left_x[...] = left3(taps_at(iota((CX, CX), 1) - iota((CX, CX), 0)))

    def some(k, _):
        for c in range(4):
            along[4 * k + c] = dot_nn(left_x[...], right3(field[4 * k + c]))
        return 0

    lax.fori_loop(0, CH // 4, some, 0)
    pack_sides(along, sides, CX, 256)
    keep.wait()


def blocks_of_16(reach):
    same = (iota((256, 256), 0) >> 4) == (iota((256, 256), 1) >> 4)
    delta = (iota((256, 256), 0) & 15) - (iota((256, 256), 1) & 15)
    return jnp.where(same, taps_at(delta + reach), 0.0)


def fix_kernel(along, above, below, sides, top, low, head_cols, tail_cols, ends):
    for ref, reach, begin, out in ((above, -16, 0, top), (below, 16, CX - 16, low)):
        more = dot3(blocks_of_16(reach).T, ref[...].reshape(256, CY)).reshape(CH, 16, CY)
        out[...] = along[:, begin : begin + 16, :] + more
        pack_sides(out, ends, 16, 256)
        head_cols[begin : begin + 16, :] = ends[:, :256]
        tail_cols[begin : begin + 16, :] = ends[:, 256:]
    head_cols[16 : CX - 16, :] = sides[16 : CX - 16, :256]
    tail_cols[16 : CX - 16, :] = sides[16 : CX - 16, 256:]


def own_y_kernel(along, top, low, out, right_y):
    right_y[...] = right3(taps_at(iota((CY, CY), 1) - iota((CY, CY), 0)))

    def some(k, _):
        for c in range(4):
            ch = 4 * k + c
            rows = jnp.concatenate([top[ch], along[ch, 16 : CX - 16, :], low[ch]], axis=0)
            out[ch] = dot_nn(left3(rows), right_y[...])
        return 0

    lax.fori_loop(0, CH // 4, some, 0)


def finish_kernel(own, side_l, side_r, out_h, work, sem):
    row = lax.axis_index("gy")
    ok_l, ok_r = row > 0, row < lax.axis_size("gy") - 1
    parts = []
    for ref, ok, reach in ((side_l, ok_l, -16), (side_r, ok_r, 16)):
        columns = jnp.where(jnp.full((CX, 256), ok), ref[...], 0.0)
        parts.append(dot3(columns, blocks_of_16(reach)))
    lane = iota((CX, 128), 1)
    copies = []
    for ch in range(CH):
        g, k = ch // 8, ch % 8
        at = slice(128 * g, 128 * g + 128)
        left, right = parts[0][:, at], parts[1][:, at]
        turn = (128 - 16 * k) % 128
        left = pltpu.roll(left, turn, 1) if turn else left
        turn = (112 - 16 * k) % 128
        right = pltpu.roll(right, turn, 1) if turn else right
        work[ch, :, 0:128] = own[ch, :, 0:128] + jnp.where(lane < 16, left, 0.0)
        work[ch, :, 128:256] = own[ch, :, 128:256] + jnp.where(lane >= 112, right, 0.0)
        copy = pltpu.make_async_copy(work.at[ch], out_h.at[ch], sem.at[ch])
        copy.start()
        copies.append(copy)
    for copy in copies:
        copy.wait()


def vmem():
    return pl.BlockSpec(memory_space=pltpu.VMEM)


def anywhere():
    return pl.BlockSpec(memory_space=pl.ANY)


def hbm():
    return pl.BlockSpec(memory_space=pltpu.HBM)


def smem():
    return pl.BlockSpec(memory_space=pltpu.SMEM)


def struct(*shape, dtype=f32):
    return jax.ShapeDtypeStruct(shape, dtype)


def params(mib):
    return pltpu.CompilerParams(vmem_limit_bytes=mib * MIB)


def cost(us, nbytes=1):
    return pl.CostEstimate(flops=int(us * 1.0e9), bytes_accessed=nbytes, transcendentals=0)


def shards(
    floe_position, floe_velocity, floe_radius, floe_thickness, tracers,
    ghost_lists, pair_first, pair_second, pair_count, cell_index,
):
    first = pair_first.reshape(64, 128)
    second = pair_second.reshape(64, 128)
    cells = cell_index.reshape(32, 128)
    radius = floe_radius.reshape(32, 128)
    thickness = floe_thickness.reshape(32, 128)
    nx, ny = lax.axis_size("gx"), lax.axis_size("gy")

    def ring(count):
        return [(i, (i + 1) % count) for i in range(count)]

    def back(count):
        return [((i + 1) % count, i) for i in range(count)]

    floe_scratch = [
        pltpu.VMEM((1, 1, 2, F), f32),
        pltpu.VMEM((1, 1, 2, F), f32),
        pltpu.VMEM((1, 1, F), f32),
    ]
    outgoing = pl.pallas_call(
        outgoing_kernel,
        in_specs=[hbm()] * 4,
        out_shape=[struct(40, 128)] * 4,
        scratch_shapes=floe_scratch
        + [
            pltpu.VMEM((1, 1, 4, G), i32),
            pltpu.VMEM((8, 128), i32),
            pltpu.SemaphoreType.DMA((4,)),
        ],
        compiler_params=params(60),
        cost_estimate=cost(1),
        name="outgoing",
    )(floe_position, floe_velocity, floe_radius, ghost_lists)
    from_below = lax.ppermute(outgoing[3], "gy", ring(ny))
    from_above = lax.ppermute(outgoing[2], "gy", back(ny))
    from_left = lax.ppermute(outgoing[1], "gx", ring(nx))
    from_right = lax.ppermute(outgoing[0], "gx", back(nx))
    ghosts = [from_below, from_above, from_left, from_right]

    packed, edges = pl.pallas_call(
        prepare_kernel,
        in_specs=[hbm()] * 7,
        out_shape=[struct(PACKED, 128), struct(16, 128, dtype=i32)],
        scratch_shapes=[
            pltpu.VMEM((64, F), bf16),
            pltpu.VMEM((128, F), bf16),
            pltpu.VMEM((32, 128), f32),
            pltpu.VMEM((32, 128), i32),
        ]
        + floe_scratch
        + [
            pltpu.VMEM((1, 1, CH, F), f32),
            pltpu.VMEM((64, 128), i32),
            pltpu.VMEM((64, 128), i32),
            pltpu.VMEM((32, 128), i32),
            pltpu.SemaphoreType.DMA((7,)),
        ],
        compiler_params=params(60),
        cost_estimate=cost(5),
        name="prepare",
    )(floe_position, floe_velocity, floe_radius, tracers, first, second, cells)

    new_velocity, values_high, values_low, sorted_pressure, head_rows, tail_rows = pl.pallas_call(
        contact_kernel,
        in_specs=[smem()] + [vmem()] * 10,
        out_shape=[
            struct(1, 1, 2, F),
            struct(CH, F),
            struct(CH, F),
            struct(32, 128),
            struct(CH, 16, CY),
            struct(CH, 16, CY),
        ],
        scratch_shapes=[pltpu.VMEM((32, 128), f32)],
        compiler_params=params(20),
        cost_estimate=cost(5),
        name="contact",
    )(
        pair_count, packed, first, second, *ghosts, radius, thickness, tracers,
    )
    above = lax.ppermute(tail_rows, "gx", ring(nx))
    below = lax.ppermute(head_rows, "gx", back(nx))

    field, along, sides = pl.pallas_call(
        grid_kernel,
        in_specs=[smem()] + [vmem()] * 5,
        out_specs=[anywhere(), vmem(), vmem()],
        out_shape=[struct(CH, CX, CY), struct(CH, CX, CY), struct(CX, 512)],
        scratch_shapes=[
            pltpu.VMEM((CH, CX, CY), f32),
            pltpu.VMEM((CX, 3 * CX), bf16),
            pltpu.VMEM((CH, F), f32),
            pltpu.VMEM((CH, F), f32),
            pltpu.SemaphoreType.DMA,
        ],
        compiler_params=params(20),
        cost_estimate=cost(10),
        name="to_grid",
    )(edges, values_high, values_low, packed, tracers, sorted_pressure)

    top, low, head_cols, tail_cols = pl.pallas_call(
        fix_kernel,
        in_specs=[vmem()] * 4,
        out_specs=[vmem()] * 4,
        out_shape=[struct(CH, 16, CY)] * 2 + [struct(CX, 256)] * 2,
        scratch_shapes=[pltpu.VMEM((16, 512), f32)],
        compiler_params=params(12),
        cost_estimate=cost(1),
        name="fix_rows",
    )(along, above, below, sides)
    side_l = lax.ppermute(tail_cols, "gy", ring(ny))
    side_r = lax.ppermute(head_cols, "gy", back(ny))

    own = pl.pallas_call(
        own_y_kernel,
        in_specs=[vmem()] * 3,
        out_specs=vmem(),
        out_shape=struct(CH, CX, CY),
        scratch_shapes=[pltpu.VMEM((3 * CY, CY), bf16)],
        compiler_params=params(12),
        cost_estimate=cost(4),
        name="own_y",
    )(along, top, low)
    smoothed = pl.pallas_call(
        finish_kernel,
        in_specs=[vmem()] * 3,
        out_specs=anywhere(),
        out_shape=struct(CH, CX, CY),
        scratch_shapes=[pltpu.VMEM((CH, CX, CY), f32), pltpu.SemaphoreType.DMA((CH,))],
        compiler_params=params(14),
        cost_estimate=cost(1),
        name="finish",
    )(own, side_l, side_r)
    return (new_velocity, field, smoothed)


def solution(mesh):
    placed = (
        P("gx", "gy", None, None),
        P("gx", "gy", None, None),
        P("gx", "gy", None),
        P("gx", "gy", None),
        P("gx", "gy", None, None),
        P("gx", "gy", None, None),
        P("gx", "gy", None),
        P("gx", "gy", None),
        P("gx", "gy"),
        P("gx", "gy", None),
    )
    return jax.shard_map(
        shards,
        mesh=mesh,
        in_specs=placed,
        out_specs=(P("gx", "gy", None, None), P(None, "gx", "gy"), P(None, "gx", "gy")),
        check_vma=False,
    )
```
